256 devices in a mesh: img: 16 (over x, y_lo, core), patch: 16 (over z, y_hi).
Axes of the slice: x: 4, y: 4 (y_hi: 2, y_lo: 2; y = y_hi * 2 + y_lo), z: 8, core: 2. Of those that a mesh axis runs over, the one named last changes fastest.
Arguments:
- img_q: bfloat16 [16, 2048, 1536], P('img', 'patch')
- fresh_kv: bfloat16 [16, 2048, 3072], P('img', 'patch'), may hold values from -6 to 6
- stale_kv: bfloat16 [16, 2048, 3072], P('img', 'patch')
- text_states: bfloat16 [16, 512, 4096], P('img', 'patch'), may hold values from -6 to 6
- ctx_weight: bfloat16 [4096, 3072], P('img', 'patch'), may hold values from -0.09375 to 0.09375
- kv_weight: bfloat16 [3072, 3072], P('img', 'patch'), may hold values from -0.109375 to 0.109375
- modulation: float32 [16, 2, 3072], P('img', None, 'patch'), may hold values from -3 to 3
- lengths: int32 [16], P('img'), may hold values from 1 to 512, as said below
Outputs:
- attended: bfloat16 [16, 2048, 1536], P('img', 'patch')
The draws below stay inside these ranges and needn't reach their ends.
Inputs may be any that keep to these rules, and one draw needn't show every extreme that they name: `lengths`: every length is at least 1 and some image's prompt has 512 live tokens.
All inputs are finite; a program needn't handle non-finite values.
Results may differ from the reference program's by a relative error of at most 0.012.
Values may be sent and summed in bfloat16 or wider, within the bound.
A program may use at most 128 MiB of HBM per device.

```python
import jax
import jax.numpy as jnp
from jax import lax

D = 3072
DT = 4096
HEADS = 12
HEAD = 128
LTEXT = 512
TOK_DEV = 128
IMAGES = 16
NTOK = 2048
N_PATCH = 16


def draw_img_q(key, part):
    key = jax.random.fold_in(key, 11)
    drawn = jax.random.normal(key, (IMAGES, NTOK, HEADS * HEAD), jnp.float32)
    return drawn.astype(jnp.bfloat16)


def draw_stale_kv(key, part):
    key = jax.random.fold_in(key, 12)
    drawn = jax.random.normal(key, (IMAGES, NTOK, 2 * HEADS * HEAD), jnp.float32)
    return drawn.astype(jnp.bfloat16)


def draw_lengths(key, part):
    key = jax.random.fold_in(key, 13)
    first_key, second_key = jax.random.split(key)
    chosen = jax.random.randint(first_key, (IMAGES,), 1, LTEXT + 1)
    picked = jax.random.randint(second_key, (), 0, IMAGES)
    return jnp.where(jnp.arange(IMAGES) == picked, LTEXT, chosen).astype(jnp.int32)


def shard_levels(own_key, dims, shards, least, top_value):
    loudness, own = 1.0, jax.random.fold_in(own_key, 6)
    for dim, parts in shards:
        draws = jnp.exp(jax.random.uniform(jax.random.fold_in(own, dim), (parts,), jnp.float32, least / len(shards), top_value / len(shards)))
        loudness = loudness * jnp.repeat(draws, dims[dim] // parts).reshape([-1 if axis == dim else 1 for axis in range(len(dims))])
    return loudness


def scatter_about(rng, shape, scale, bound, cuts=(), kind=jnp.bfloat16):
    loudness = shard_levels(rng, shape, cuts, -0.22, 0.18) if cuts else 1.0
    entries = jax.random.normal(rng, shape, jnp.float32) * scale * loudness
    return jnp.minimum(jnp.maximum(entries, -bound), bound).astype(kind)


def setup_inputs(seed: int = 0) -> dict:
    seeds = jax.random.split(jax.random.key(seed), 9)
    return {
        "img_q": draw_img_q(jax.random.fold_in(seeds[8], 71), 0),
        "fresh_kv": scatter_about(seeds[1], (IMAGES, NTOK, 2 * HEADS * HEAD), 1.0, 6.0, ((0, 16), (1, 16))),
        "stale_kv": draw_stale_kv(jax.random.fold_in(seeds[8], 71), 0),
        "text_states": scatter_about(seeds[3], (IMAGES, LTEXT, DT), 1.0, 6.0, ((0, 16), (1, 16))),
        "ctx_weight": scatter_about(seeds[4], (DT, D), DT ** -0.5, 0.09375, ((0, 16), (1, 16))),
        "kv_weight": scatter_about(seeds[5], (2 * HEADS * HEAD, D), D ** -0.5, 0.109375, ((0, 16), (1, 16))),
        "modulation": scatter_about(seeds[6], (IMAGES, 2, D), 0.5, 3.0, ((0, 16), (2, 16)), jnp.float32),
        "lengths": draw_lengths(jax.random.fold_in(seeds[8], 71), 0),
    }


def reference(img_q, fresh_kv, stale_kv, text_states, ctx_weight, kv_weight, modulation, lengths):
    hd_width = HEADS * HEAD
    scaling = 1.0 / HEAD ** 0.5

    def one_image(inputs):
        queries, fresh, stale, prompt, modul, length = inputs
        context = jnp.dot(prompt, ctx_weight, preferred_element_type=jnp.float32)
        average = lax.optimization_barrier(jnp.sum(context, -1, keepdims=True)) / D
        variance = lax.optimization_barrier(jnp.sum(context * context, -1, keepdims=True)) / D - average * average
        normed = ((context - average) * lax.rsqrt(variance + 1e-06) * (1.0 + modul[0]) + modul[1]).astype(jnp.bfloat16)
        text_kv = lax.dot_general(normed, kv_weight, (((1,), (1,)), ((), ())), preferred_element_type=jnp.float32).astype(jnp.bfloat16)
        text_usable = jnp.arange(LTEXT, dtype=jnp.int32) < length
        usable = jnp.concatenate([text_usable, jnp.ones((NTOK,), jnp.bool_)])

        def query_block(index):
            begin = (index * TOK_DEV).astype(jnp.int32)
            block_q = lax.dynamic_slice_in_dim(queries, begin, TOK_DEV, 0)
            block_fresh = lax.dynamic_slice_in_dim(fresh, begin, TOK_DEV, 0)
            image_kv = lax.dynamic_update_slice_in_dim(stale, block_fresh, begin, 0)
            every_kv = jnp.concatenate([text_kv, image_kv], 0).astype(jnp.float32)
            key_heads = every_kv[:, :hd_width].reshape(-1, HEADS, HEAD)
            value_heads = every_kv[:, hd_width:].reshape(-1, HEADS, HEAD)
            query_heads = block_q.astype(jnp.float32).reshape(TOK_DEV, HEADS, HEAD)
            scores = jnp.einsum('rhd,nhd->rhn', query_heads, key_heads) * scaling
            scores = jnp.where(usable[None, None, :], scores, -jnp.inf)
            highest = lax.optimization_barrier(jnp.max(scores, -1, keepdims=True))
            weights = jnp.exp(scores - highest)
            denom = lax.optimization_barrier(jnp.sum(weights, -1))
            rounded = lax.optimization_barrier(weights.astype(jnp.bfloat16)).astype(jnp.float32)
            mixed = jnp.einsum('rhn,nhd->rhd', rounded, value_heads) / denom[..., None]
            return mixed.reshape(TOK_DEV, hd_width).astype(jnp.bfloat16)
        return lax.map(query_block, jnp.arange(N_PATCH, dtype=jnp.int32)).reshape(NTOK, hd_width)
    return lax.map(one_image, (img_q, fresh_kv, stale_kv, text_states, modulation, lengths))
```

```python
import functools
import math

import jax
import jax.numpy as jnp
from jax import lax
from jax.experimental import pallas as pl
from jax.experimental.pallas import tpu as pltpu
from jax.sharding import PartitionSpec as P

D = 3072
HEAD = 128
NX, NY, NZ = 4, 4, 8
HALF = 768
NH = 6
MESH = pl.DeviceIdType.MESH
BF = jnp.bfloat16
F32 = jnp.float32


def device(x, y, z, core):
    return ((x * 2 + y % 2) * 2 + core, z * 2 + y // 2)


class Net:
    def __init__(self, send, recv):
        self.send, self.recv, self.used, self.copies = send, recv, 0, []

    def copy(self, src, dst, to):
        n = self.used
        self.used += 1
        c = pltpu.make_async_remote_copy(
            src_ref=src,
            dst_ref=dst,
            send_sem=self.send.at[n],
            recv_sem=self.recv.at[n],
            device_id=to,
            device_id_type=MESH,
        )
        self.copies.append(c)
        return c

    def drain(self):
        for c in self.copies:
            c.wait_send()


class Ring:
    def __init__(self, net, slot, rows, left, right, first=None, by_origin=False):
        h = rows // 2
        self.step = {}
        for s in range(4):
            for way in (0, 1):
                if way == 0:
                    a, b, to, part = s, s + 1, right, pl.ds(0, h)
                else:
                    a, b, to, part = (8 - s) % 8, 7 - s, left, pl.ds(h, h)
                src, dst = slot(a), slot(a if by_origin else b)
                if s == 0 and first is not None:
                    src = first
                if s == 3:
                    src, dst = src.at[part], dst.at[part]
                self.step[way, s] = net.copy(src, dst, to)

    def start(self):
        self.step[0, 0].start()
        self.step[1, 0].start()

    def forward(self, s):
        for way in (0, 1):
            self.step[way, s - 1].wait_recv()
            self.step[way, s].start()

    def finish(self):
        for way in (0, 1):
            self.step[way, 3].wait_recv()


def kernel(
    q_hbm, fresh_hbm, stale_hbm, text_hbm, cw_ref, kw_ref, mod_ref, len_ref, out_ref,
    tx, wy, ky, wx, kx, mb, st, pt, rs_out, rs_in, tkv, tk, tv, sk, sv, qb, fk, fv,
    acc, mx, dn, ob, ob_in, send_sem, recv_sem, loc_sem,
):
    img, patch = lax.axis_index("img"), lax.axis_index("patch")
    x, core = img // 4, img % 2
    z, h = patch // 2, patch % 2
    y = h * 2 + (img // 2) % 2
    right, left = device(x, y, (z + 1) % NZ, core), device(x, y, (z + 7) % NZ, core)
    zs = {k: device(x, y, (z + k) % NZ, core) for k in range(1, NZ)}
    xs = {k: device((x + k) % NX, y, z, core) for k in range(1, NX)}
    ys = {k: device(x, (y + k) % NY, z, core) for k in range(1, NY)}
    other = device(x, y, z, 1 - core)
    opposite = ys[2]
    mine, theirs = h * HALF, (1 - h) * HALF
    net = Net(send_sem, recv_sem)

    def at_z(k):
        return (z + NZ - k) % NZ

    def cols(ref, at):
        return ref.at[0, :, pl.ds(pl.multiple_of(at, 128), HALF)]

    locals_ = []

    def local(src, dst):
        c = pltpu.make_async_copy(src, dst, loc_sem.at[len(locals_)])
        locals_.append(c)
        c.start()
        return c

    c_text = local(text_hbm.at[0], tx.at[z])
    c_q = local(cols(q_hbm, mine), qb.at[0])
    c_fk = local(cols(fresh_hbm, mine), fk.at[0])
    c_fv = local(cols(fresh_hbm, D // 2 + mine), fv.at[0])
    c_sk = local(cols(stale_hbm, mine), sk.at[0, 0])
    c_sv = local(cols(stale_hbm, D // 2 + mine), sv.at[0, 0])

    w = cw_ref[...]
    wy[y, 0:256] = w[:, 0:128]
    wy[y, 256:384] = jnp.concatenate([w[0:128, 128:192], w[128:256, 128:192]], axis=1)
    w = kw_ref[...]
    ky[y, 0:192] = w[:, 0:128]
    ky[y, 192:288] = jnp.concatenate([w[0:96, 128:192], w[96:192, 128:192]], axis=1)
    mb[h, 0:2, 0:192] = mod_ref[0]

    barrier = pltpu.get_barrier_semaphore()
    peers = [*zs.values(), *xs.values(), *ys.values(), other]
    for d in peers:
        pl.semaphore_signal(barrier, inc=1, device_id=d, device_id_type=MESH)
    pl.semaphore_wait(barrier, len(peers))

    text = Ring(net, lambda k: tx.at[at_z(k)], 32, left, right, text_hbm.at[0], True)
    text.start()
    wy_c = {k: net.copy(wy.at[y], wy.at[y], ys[k]) for k in ys}
    ky_c = {k: net.copy(ky.at[y], ky.at[y], ys[k]) for k in ys}
    for c in wy_c.values():
        c.start()
    m_c = net.copy(mb.at[h], mb.at[h], opposite)
    m_c.start()
    for c in ky_c.values():
        c.start()

    s_opp = [
        net.copy(cols(stale_hbm, theirs), sk.at[0, 1], opposite),
        net.copy(cols(stale_hbm, D // 2 + theirs), sv.at[0, 1], opposite),
    ]
    qf_opp = [
        net.copy(cols(q_hbm, theirs), qb.at[1], opposite),
        net.copy(cols(fresh_hbm, theirs), fk.at[1], opposite),
        net.copy(cols(fresh_hbm, D // 2 + theirs), fv.at[1], opposite),
    ]
    stale = [
        Ring(net, lambda k, b=b, r=r: b.at[k, r], 128, left, right, first=f)
        for r in (0, 1)
        for b, f in (
            (sk, cols(stale_hbm, mine) if r == 0 else None),
            (sv, cols(stale_hbm, D // 2 + mine) if r == 0 else None),
        )
    ]

    def pair(tiles, rows, out):
        for lo in (0, 1):
            a, b = tiles[lo], tiles[2 + lo]
            out[x, core, lo, 0] = a[0:rows]
            out[x, core, lo, 1] = b[0:rows]
            a, b = a[rows:], b[rows:]
            out[x, core, lo, 2, 0 : rows // 2] = jnp.concatenate([a[:, 0:64], b[:, 0:64]], axis=1)
            out[x, core, lo, 2, rows // 2 :] = jnp.concatenate([a[:, 64:], b[:, 64:]], axis=1)

    def spread(got, tiles, rows, out):
        for c in got.values():
            c.wait_recv()
        pair(tiles, rows, out)
        to_x = {k: net.copy(out.at[x, core], out.at[x, core], xs[k]) for k in xs}
        for c in to_x.values():
            c.start()
        to_core = [net.copy(out.at[x, core], out.at[x, core], other)]
        to_core[0].start()
        for k in xs:
            at = (x + NX - k) % NX
            to_core.append(net.copy(out.at[at, core], out.at[at, core], other))
        return to_x, to_core

    def pass_on(to_x, to_core, k):
        to_x[k].wait_recv()
        to_core[k].start()

    wx_x, wx_core = spread(wy_c, wy, 256, wx)
    for c in s_opp:
        c.start()
    text.forward(1)
    stale[0].start()
    stale[1].start()
    for c in qf_opp:
        c.start()
    kx_x, kx_core = spread(ky_c, ky, 192, kx)
    text.forward(2)
    pass_on(wx_x, wx_core, 1)
    pass_on(wx_x, wx_core, 3)
    text.forward(3)
    pass_on(wx_x, wx_core, 2)
    stale[0].forward(1)
    stale[1].forward(1)
    for c in s_opp:
        c.wait_recv()
    stale[2].start()
    stale[3].start()
    text.finish()
    c_text.wait()
    for c in wx_core:
        c.wait_recv()

    ctx = jnp.zeros((256, 384), F32)
    for i in range(NX):
        rhs = jnp.concatenate(
            [
                jnp.concatenate([wx[i, c, lo, b] for b in range(3)], axis=1)
                for lo in (0, 1)
                for c in (0, 1)
            ],
            axis=0,
        )
        lhs = tx[:, :, i * 1024 : (i + 1) * 1024].reshape(256, 1024)
        ctx = ctx + jnp.dot(lhs, rhs, preferred_element_type=F32)
    lane = lax.broadcasted_iota(jnp.int32, (256, 128), 1)
    s1 = jnp.sum(ctx, -1, keepdims=True)
    s2 = jnp.sum(ctx * ctx, -1, keepdims=True)
    both = jnp.where(lane == 0, s1, jnp.where(lane == 1, s2, 0.0))
    st[0] = jnp.transpose(both)[0:8]
    st_c = [net.copy(st.at[0], st.at[k], zs[k]) for k in zs]
    for c in st_c:
        c.start()
    pass_on(kx_x, kx_core, 1)
    pass_on(kx_x, kx_core, 3)
    pass_on(kx_x, kx_core, 2)
    m_c.wait_recv()
    low = lax.broadcasted_iota(jnp.int32, (8, 128), 1) < 64
    ma, mb_ = mb[0], mb[1]
    tail = jnp.where(low, ma[:, 128:256], pltpu.roll(mb_[:, 128:256], 64, 1))
    modul = jnp.concatenate([ma[:, 0:128], mb_[:, 0:128], tail], axis=1)
    for c in st_c:
        c.wait_recv()
    tot = st[0]
    for k in range(1, NZ):
        tot = tot + st[k]
    tot = jnp.transpose(jnp.concatenate([tot, jnp.zeros((120, 256), F32)], axis=0))
    average = tot[:, 0:1] / D
    variance = tot[:, 1:2] / D - average * average
    normed = (
        (ctx - average) * lax.rsqrt(variance + 1e-06) * (1.0 + modul[0:1]) + modul[1:2]
    ).astype(BF)
    for c in kx_core:
        c.wait_recv()
    for i in range(NX):
        for lo in (0, 1):
            rhs = jnp.concatenate(
                [jnp.concatenate([kx[i, c, lo, b] for b in range(3)], axis=1) for c in (0, 1)],
                axis=0,
            )
            part = lax.dot_general(
                normed, rhs, (((1,), (1,)), ((), ())), preferred_element_type=F32
            )
            at = (i * 2 + lo) * 384
            pt[:, :, at : at + 384] = part.reshape(NZ, 32, 384)

    steps = {}
    for way in (0, 1):
        to, half = (left, pl.ds(0, 16)) if way == 0 else (right, pl.ds(16, 16))
        for n in range(4):
            src, dst = rs_out.at[way, n], rs_in.at[way, n]
            if n == 0:
                src, dst = src.at[half], dst.at[half]
            steps[way, n] = net.copy(src, dst, to)

    def sum_step(n):
        for way in (0, 1):
            slot = 4 - n if way == 0 else 4 + n
            if n == 0:
                part = slice(0, 16) if way == 0 else slice(16, 32)
                rs_out[way, 0, part] = pt[at_z(slot), part].astype(BF)
            else:
                steps[way, n - 1].wait_recv()
                if n == 1:
                    part = slice(0, 16) if way == 0 else slice(16, 32)
                    rest = slice(16, 32) if way == 0 else slice(0, 16)
                    rs_out[way, 1, part] = (pt[at_z(slot), part] + rs_in[way, 0, part]).astype(BF)
                    rs_out[way, 1, rest] = pt[at_z(slot), rest].astype(BF)
                else:
                    rs_out[way, n] = (pt[at_z(slot)] + rs_in[way, n - 1]).astype(BF)
            steps[way, n].start()

    def stale_step(s):
        for r in stale:
            r.forward(s)

    sum_step(0)
    stale[2].forward(1)
    stale[3].forward(1)
    sum_step(1)
    stale[0].forward(2)
    stale[1].forward(2)
    sum_step(2)
    sum_step(3)
    stale[2].forward(2)
    stale[3].forward(2)
    steps[0, 3].wait_recv()
    steps[1, 3].wait_recv()
    tkv[...] = (pt[z] + rs_in[0, 3] + rs_in[1, 3]).astype(BF)
    t_opp = [
        net.copy(tkv.at[:, pl.ds(pl.multiple_of(o + theirs, 128), HALF)], b.at[0, 1], opposite)
        for o, b in ((0, tk), (D // 2, tv))
    ]
    for c in t_opp:
        c.start()
    tk[0, 0] = tkv[:, pl.ds(pl.multiple_of(mine, 128), HALF)]
    tv[0, 0] = tkv[:, pl.ds(pl.multiple_of(D // 2 + mine, 128), HALF)]
    tring = [
        Ring(net, lambda k, b=b, r=r: b.at[k, r], 32, left, right)
        for r in (0, 1)
        for b in (tk, tv)
    ]
    tring[0].start()
    tring[1].start()
    for c in t_opp:
        c.wait_recv()
    tring[2].start()
    tring[3].start()

    c2 = math.log2(math.e) / math.sqrt(HEAD)
    contract = (((1,), (1,)), ((), ()))

    def head(n):
        return pl.ds(pl.multiple_of(n * HEAD, HEAD), HEAD)

    def scores(q, k):
        return lax.dot_general(q, k, contract, preferred_element_type=F32) * c2

    for c in (c_q, c_fk, c_fv, c_sk, c_sv):
        c.wait()
    for c in qf_opp:
        c.wait_recv()

    def first_block(n, _):
        for r in (0, 1):
            k = jnp.concatenate([fk[r, :, head(n)], sk[0, 1 - r, :, head(n)]], axis=0)
            v = jnp.concatenate([fv[r, :, head(n)], sv[0, 1 - r, :, head(n)]], axis=0)
            s = scores(qb[r, :, head(n)], k)
            m = jnp.max(s, -1, keepdims=True)
            p = jnp.exp2(s - m)
            rows = pl.ds(r * 128, 128)
            mx[n, rows] = jnp.broadcast_to(m, (128, 128))
            dn[n, rows] = jnp.broadcast_to(jnp.sum(p, -1, keepdims=True), (128, 128))
            acc[n, rows] = jnp.dot(p.astype(BF), v, preferred_element_type=F32)
        return 0

    def attend(keys, values, mask=None):
        def body(n, _):
            q = qb[:, :, head(n)].reshape(256, HEAD)
            k = jnp.concatenate([b[..., head(n)].reshape(-1, HEAD) for b in keys], axis=0)
            v = jnp.concatenate([b[..., head(n)].reshape(-1, HEAD) for b in values], axis=0)
            s = scores(q, k)
            if mask is not None:
                s = jnp.where(mask, s, -jnp.inf)
            old = mx[n]
            m = jnp.maximum(old, jnp.max(s, -1, keepdims=True))
            p = jnp.exp2(s - m[:, 0:1])
            alpha = jnp.exp2(old - m)
            mx[n] = m
            dn[n] = dn[n] * alpha + jnp.sum(p, -1, keepdims=True)
            acc[n] = acc[n] * alpha + jnp.dot(p.astype(BF), v, preferred_element_type=F32)
            return 0

        lax.fori_loop(0, NH, body, 0)

    def attend_slots(*slots):
        attend([sk.at[k] for k in slots], [sv.at[k] for k in slots])

    def tring_step(s):
        for r in tring:
            r.forward(s)

    lax.fori_loop(0, NH, first_block, 0)
    tring_step(1)
    attend_slots(1, 7)
    tring_step(2)
    stale[0].forward(3)
    stale[1].forward(3)
    tring_step(3)
    stale[2].forward(3)
    stale[3].forward(3)
    attend_slots(2, 6)
    attend_slots(3, 5)
    for r in tring:
        r.finish()
    at = lax.broadcasted_iota(jnp.int32, (1, 512), 1)
    slot, rel, row = at // 64, (at // 32) % 2, at % 32
    position = at_z(slot) * 64 + jnp.where(rel == 0, h, 1 - h) * 32 + row
    attend([tk], [tv], position < len_ref[0])
    for r in stale:
        r.finish()
    attend_slots(4)

    def close(r, out):
        for n in range(NH):
            rows = pl.ds(r * 128, 128)
            out[:, n * HEAD : (n + 1) * HEAD] = (acc[n, rows] / dn[n, rows]).astype(BF)

    close(1, ob)
    o_c = net.copy(ob, ob_in, opposite)
    o_c.start()
    for n in range(NH):
        rows = pl.ds(0, 128)
        out_ref[0, :, head(h * NH + n)] = (acc[n, rows] / dn[n, rows]).astype(BF)
    o_c.wait_recv()
    out_ref[0, :, pl.ds(pl.multiple_of(theirs, 128), HALF)] = ob_in[...]
    net.drain()


N_COPIES = 160


def per_device(img_q, fresh_kv, stale_kv, text_states, ctx_weight, kv_weight, modulation, lengths):
    hbm = pl.BlockSpec(memory_space=pl.ANY)
    vmem = pl.BlockSpec(memory_space=pltpu.VMEM)
    smem = pl.BlockSpec(memory_space=pltpu.SMEM)
    return pl.pallas_call(
        kernel,
        out_shape=jax.ShapeDtypeStruct((1, 128, 1536), BF),
        in_specs=[hbm, hbm, hbm, hbm, vmem, vmem, vmem, smem],
        out_specs=vmem,
        scratch_shapes=[
            pltpu.VMEM((NZ, 32, 4096), BF),
            pltpu.VMEM((NY, 384, 128), BF),
            pltpu.VMEM((NY, 288, 128), BF),
            pltpu.VMEM((NX, 2, 2, 3, 256, 128), BF),
            pltpu.VMEM((NX, 2, 2, 3, 192, 128), BF),
            pltpu.VMEM((2, 8, 256), F32),
            pltpu.VMEM((NZ, 8, 256), F32),
            pltpu.VMEM((NZ, 32, D), F32),
            pltpu.VMEM((2, 4, 32, D), BF),
            pltpu.VMEM((2, 4, 32, D), BF),
            pltpu.VMEM((32, D), BF),
            pltpu.VMEM((NZ, 2, 32, HALF), BF),
            pltpu.VMEM((NZ, 2, 32, HALF), BF),
            pltpu.VMEM((NZ, 2, 128, HALF), BF),
            pltpu.VMEM((NZ, 2, 128, HALF), BF),
            pltpu.VMEM((2, 128, HALF), BF),
            pltpu.VMEM((2, 128, HALF), BF),
            pltpu.VMEM((2, 128, HALF), BF),
            pltpu.VMEM((NH, 256, HEAD), F32),
            pltpu.VMEM((NH, 256, HEAD), F32),
            pltpu.VMEM((NH, 256, HEAD), F32),
            pltpu.VMEM((128, HALF), BF),
            pltpu.VMEM((128, HALF), BF),
            pltpu.SemaphoreType.DMA((N_COPIES,)),
            pltpu.SemaphoreType.DMA((N_COPIES,)),
            pltpu.SemaphoreType.DMA((8,)),
        ],
        compiler_params=pltpu.CompilerParams(
            collective_id=0, has_side_effects=True, vmem_limit_bytes=50 << 20
        ),
    )(img_q, fresh_kv, stale_kv, text_states, ctx_weight, kv_weight, modulation, lengths)


def solution(mesh):
    in_specs = (
        P("img", "patch", None),
        P("img", "patch", None),
        P("img", "patch", None),
        P("img", "patch", None),
        P("img", "patch"),
        P("img", "patch"),
        P("img", None, "patch"),
        P("img"),
    )
    return jax.shard_map(
        per_device,
        mesh=mesh,
        in_specs=in_specs,
        out_specs=P("img", "patch", None),
        check_vma=False,
    )
```

```python
import functools
import math

import jax
import jax.numpy as jnp
from jax import lax
from jax.experimental import pallas as pl
from jax.experimental.pallas import tpu as pltpu
from jax.sharding import PartitionSpec as P

D = 3072
HEAD = 128
NX, NY, NZ = 4, 4, 8
HALF = 768
NH = 6
MESH = pl.DeviceIdType.MESH
BF = jnp.bfloat16
F32 = jnp.float32


def device(x, y, z, core):
    return ((x * 2 + y % 2) * 2 + core, z * 2 + y // 2)


class Net:
    def __init__(self, send, recv):
        self.send, self.recv, self.used, self.copies = send, recv, 0, []

    def copy(self, src, dst, to):
        n = self.used
        self.used += 1
        c = pltpu.make_async_remote_copy(
            src_ref=src,
            dst_ref=dst,
            send_sem=self.send.at[n],
            recv_sem=self.recv.at[n],
            device_id=to,
            device_id_type=MESH,
        )
        self.copies.append(c)
        return c

    def drain(self):
        for c in self.copies:
            c.wait_send()


class Ring:
    def __init__(self, net, slot, far, left, right, first=None, by_origin=False):
        self.step = {}
        for s in range(4):
            for way in (far, 1 - far):
                if s == 3 and way != far:
                    continue
                a, b, to = (s, s + 1, right) if way == 0 else ((8 - s) % 8, 7 - s, left)
                src, dst = slot(a), slot(a if by_origin else b)
                if s == 0 and first is not None:
                    src = first
                self.step[s, way] = net.copy(src, dst, to)

    def start(self):
        for way in (0, 1):
            self.step[0, way].start()

    def forward(self, s):
        for way in (0, 1):
            self.step[s - 1, way].wait_recv()
            if (s, way) in self.step:
                self.step[s, way].start()

    def finish(self):
        for way in (0, 1):
            if (3, way) in self.step:
                self.step[3, way].wait_recv()


def kernel(
    q_hbm, fresh_hbm, stale_hbm, text_hbm, cw_hbm, kw_hbm, mod_hbm, len_ref, out_ref,
    tx, kraw, kpack, w0, w1, k0, k1, mraw, mb, st, pt, rs_out, rs_in, tkv, tk, tv, sk, sv, qb, fk, fv,
    acc, mx, dn, ob, ob_in, send_sem, recv_sem, loc_sem,
):
    img, patch = lax.axis_index("img"), lax.axis_index("patch")
    x, core = img // 4, img % 2
    z, h = patch // 2, patch % 2
    y = h * 2 + (img // 2) % 2
    right, left = device(x, y, (z + 1) % NZ, core), device(x, y, (z + 7) % NZ, core)
    zs = {k: device(x, y, (z + k) % NZ, core) for k in range(1, NZ)}
    xs = {k: device((x + k) % NX, y, z, core) for k in range(1, NX)}
    ys = {k: device(x, (y + k) % NY, z, core) for k in range(1, NY)}
    other = device(x, y, z, 1 - core)
    opposite = ys[2]
    mine, theirs = h * HALF, (1 - h) * HALF
    net = Net(send_sem, recv_sem)

    barrier = pltpu.get_barrier_semaphore()
    peers = [right, left, *xs.values(), *ys.values(), other]
    for d in peers:
        pl.semaphore_signal(barrier, inc=1, device_id=d, device_id_type=MESH)

    def at_z(k):
        return (z + NZ - k) % NZ

    def cols(ref, at):
        return ref.at[0, :, pl.ds(pl.multiple_of(at, 128), HALF)]

    locals_ = []

    def local(src, dst):
        c = pltpu.make_async_copy(src, dst, loc_sem.at[len(locals_)])
        locals_.append(c)
        c.start()
        return c

    def text_cols(p):
        return text_hbm.at[0, :, pl.ds(p * 2048, 2048)]

    c_kw = local(kw_hbm, kraw)
    c_mod = local(mod_hbm.at[0], mraw)
    cw = [cw_hbm.at[pl.ds(p * 96, 96)] for p in (0, 1)]
    c_cw = [local(cw[0], w0.at[x, core, y]), local(cw[1], w1.at[y, core, x])]
    c_text = [local(text_cols(p), tx.at[p, z]) for p in (0, 1)]
    c_img = [
        local(cols(q_hbm, mine), qb.at[0]),
        local(cols(fresh_hbm, mine), fk.at[0]),
        local(cols(fresh_hbm, D // 2 + mine), fv.at[0]),
        local(cols(stale_hbm, mine), sk.at[0, 0]),
        local(cols(stale_hbm, D // 2 + mine), sv.at[0, 0]),
    ]
    c_kw.wait()
    w = kraw[...]
    kpack[0:192] = w[:, 0:128]
    kpack[192:288] = jnp.concatenate([w[0:96, 128:192], w[96:192, 128:192]], axis=1)
    k0[x, core, y] = kpack[0:144]
    k1[y, core, x] = kpack[144:288]
    c_mod.wait()
    mb[h, 0:2, 0:192] = mraw[...]
    pl.semaphore_wait(barrier, len(peers))

    text = [Ring(net, lambda k, p=p: tx.at[p, at_z(k)], p, left, right, text_cols(p), True) for p in (0, 1)]

    class Spread:
        def __init__(self, buf, i, j, own, first, second):
            self.first = {k: net.copy(own, buf.at[i, core, j], first[k]) for k in first}
            self.second = {k: net.copy(buf.at[i, core], buf.at[i, core], second[k]) for k in second}
            self.core = {k: net.copy(buf.at[(i + 4 - k) % 4, core], buf.at[(i + 4 - k) % 4, core], other) for k in range(4)}

        def start(self):
            for c in self.first.values():
                c.start()

        def middle(self):
            for c in self.first.values():
                c.wait_recv()
            for k in (2, 1, 3):
                self.second[k].start()
            self.core[0].start()

        def pass_on(self):
            for k in (1, 3, 2):
                self.second[k].wait_recv()
                self.core[k].start()

        def finish(self):
            for c in self.core.values():
                c.wait_recv()

    ws = [Spread(w0, x, y, cw[0], ys, xs), Spread(w1, y, x, cw[1], xs, ys)]
    ks = [
        Spread(k0, x, y, kpack.at[pl.ds(0, 144)], ys, xs),
        Spread(k1, y, x, kpack.at[pl.ds(144, 144)], xs, ys),
    ]
    m_c = net.copy(mb.at[h], mb.at[h], opposite)
    s_opp = [
        net.copy(cols(stale_hbm, theirs), sk.at[0, 1], opposite),
        net.copy(cols(stale_hbm, D // 2 + theirs), sv.at[0, 1], opposite),
    ]
    qf_opp = [
        net.copy(cols(q_hbm, theirs), qb.at[1], opposite),
        net.copy(cols(fresh_hbm, theirs), fk.at[1], opposite),
        net.copy(cols(fresh_hbm, D // 2 + theirs), fv.at[1], opposite),
    ]
    stale = [
        Ring(net, lambda k, b=b, r=r: b.at[k, r], far, left, right, f)
        for r in (0, 1)
        for far, b, f in (
            (0, sk, cols(stale_hbm, mine) if r == 0 else None),
            (1, sv, cols(stale_hbm, D // 2 + mine) if r == 0 else None),
        )
    ]
    stale_work = []
    for s in range(4):
        for n, r in enumerate(stale):
            if s == 0:
                stale_work.append((r.start, s_opp[n - 2] if n >= 2 else None))
            else:
                stale_work.append((functools.partial(r.forward, s), None))

    def pump(n):
        for _ in range(min(n, len(stale_work))):
            go, before = stale_work.pop(0)
            if before is not None:
                before.wait_recv()
            go()

    def each(things, method, *args):
        for t in things:
            getattr(t, method)(*args)

    def tile(a, b, i, c, lo):
        return [jnp.concatenate([a[i, c, t], b[t, c, i]], axis=0) for t in (lo, 2 + lo)]

    held = {}

    def context():
        each(c_text, "wait")
        ctx = jnp.zeros((256, 384), F32)
        for i in range(NX):
            blocks = []
            for lo in (0, 1):
                for c in (0, 1):
                    a, b = tile(w0, w1, i, c, lo)
                    blocks.append(jnp.concatenate([a[0:128], b[0:128], a[128:], b[128:]], axis=0))
            rhs = jnp.concatenate(blocks, axis=1)
            lhs = tx[i // 2, :, :, (i % 2) * 1024 : (i % 2 + 1) * 1024].reshape(256, 1024)
            ctx = ctx + lax.dot_general(
                lhs, rhs, (((1,), (1,)), ((), ())), preferred_element_type=F32
            )
        lane = lax.broadcasted_iota(jnp.int32, (256, 128), 1)
        s1 = jnp.sum(ctx, -1, keepdims=True)
        s2 = jnp.sum(ctx * ctx, -1, keepdims=True)
        both = jnp.where(lane == 0, s1, jnp.where(lane == 1, s2, 0.0))
        st[0] = jnp.transpose(both)[0:8]
        st_c = [net.copy(st.at[0], st.at[k], zs[k]) for k in zs]
        for c in st_c:
            c.start()
        held.update(ctx=ctx, st_c=st_c)

    def norm():
        ctx, st_c = held["ctx"], held["st_c"]
        m_c.wait_recv()
        low = lax.broadcasted_iota(jnp.int32, (8, 128), 1) < 64
        ma, mb_ = mb[0], mb[1]
        tail = jnp.where(low, ma[:, 128:256], pltpu.roll(mb_[:, 128:256], 64, 1))
        modul = jnp.concatenate([ma[:, 0:128], mb_[:, 0:128], tail], axis=1)
        for c in st_c:
            c.wait_recv()
        tot = st[0]
        for k in range(1, NZ):
            tot = tot + st[k]
        tot = jnp.transpose(jnp.concatenate([tot, jnp.zeros((120, 256), F32)], axis=0))
        average = tot[:, 0:1] / D
        variance = tot[:, 1:2] / D - average * average
        normed = (
            (ctx - average) * lax.rsqrt(variance + 1e-06) * (1.0 + modul[0:1]) + modul[1:2]
        ).astype(BF)
        held["normed"] = normed

    def partial_kv():
        normed = held["normed"]
        for i in range(NX):
            for lo in (0, 1):
                blocks = []
                for c in (0, 1):
                    a, b = tile(k0, k1, i, c, lo)
                    ra, rb = a[192:], b[192:]
                    last = jnp.concatenate(
                        [
                            jnp.concatenate([ra[:, 0:64], rb[:, 0:64]], axis=1),
                            jnp.concatenate([ra[:, 64:], rb[:, 64:]], axis=1),
                        ],
                        axis=0,
                    )
                    blocks.append(jnp.concatenate([a[0:192], b[0:192], last], axis=1))
                part = lax.dot_general(
                    normed,
                    jnp.concatenate(blocks, axis=0),
                    (((1,), (1,)), ((), ())),
                    preferred_element_type=F32,
                )
                at = (i * 2 + lo) * 384
                pt[:, :, at : at + 384] = part.reshape(NZ, 32, 384)

    parts = (slice(0, D // 2), slice(D // 2, D))
    steps = {}
    for n in range(4):
        for way in (0, 1):
            for p in (way, 1 - way):
                if n > 0 or p == way:
                    to = left if way == 0 else right
                    steps[n, way, p] = net.copy(rs_out.at[way, n, p], rs_in.at[way, n, p], to)

    def sum_step(n):
        for p in (0, 1):
            for way in (0, 1):
                if (n, way, p) not in steps:
                    continue
                term = pt[at_z(4 - n if way == 0 else 4 + n), :, parts[p]]
                if (n - 1, way, p) in steps:
                    steps[n - 1, way, p].wait_recv()
                    term = term + rs_in[way, n - 1, p]
                rs_out[way, n, p] = term.astype(BF)
                steps[n, way, p].start()

    tring = [
        Ring(net, lambda k, b=b, r=r: b.at[k, r], far, left, right)
        for r in (0, 1)
        for far, b in ((0, tk), (1, tv))
    ]
    t_opp = []

    def sum_end():
        for p, b in ((0, tk), (1, tv)):
            for way in (0, 1):
                steps[3, way, p].wait_recv()
            tkv[p] = (pt[z, :, parts[p]] + rs_in[0, 3, p] + rs_in[1, 3, p]).astype(BF)
            c = net.copy(tkv.at[p, :, pl.ds(pl.multiple_of(theirs, 128), HALF)], b.at[0, 1], opposite)
            c.start()
            t_opp.append(c)
            b[0, 0] = tkv[p, :, pl.ds(pl.multiple_of(mine, 128), HALF)]
            tring[p].start()

    def ring_opposite():
        for p in (0, 1):
            t_opp[p].wait_recv()
            tring[2 + p].start()

    c2 = math.log2(math.e) / math.sqrt(HEAD)
    contract = (((1,), (1,)), ((), ()))

    def head(n):
        return pl.ds(pl.multiple_of(n * HEAD, HEAD), HEAD)

    def scores(q, k):
        return lax.dot_general(q, k, contract, preferred_element_type=F32) * c2

    def first_block(n, _):
        for r in (0, 1):
            k = jnp.concatenate([fk[r, :, head(n)], sk[0, 1 - r, :, head(n)]], axis=0)
            v = jnp.concatenate([fv[r, :, head(n)], sv[0, 1 - r, :, head(n)]], axis=0)
            s = scores(qb[r, :, head(n)], k)
            m = jnp.max(s, -1, keepdims=True)
            p = jnp.exp2(s - m)
            rows = pl.ds(r * 128, 128)
            mx[n, rows] = jnp.broadcast_to(m, (128, 128))
            dn[n, rows] = jnp.broadcast_to(jnp.sum(p, -1, keepdims=True), (128, 128))
            acc[n, rows] = jnp.dot(p.astype(BF), v, preferred_element_type=F32)
        return 0

    def attend(keys, values, mask=None, block=None, heads=(0, NH)):
        rows = slice(None) if block is None else pl.ds(block * 128, 128)

        def body(n, _):
            if block is None:
                q = qb[:, :, head(n)].reshape(256, HEAD)
            else:
                q = qb[block, :, head(n)]
            k = jnp.concatenate([b[..., head(n)].reshape(-1, HEAD) for b in keys], axis=0)
            v = jnp.concatenate([b[..., head(n)].reshape(-1, HEAD) for b in values], axis=0)
            s = scores(q, k)
            if mask is not None:
                s = jnp.where(mask, s, -jnp.inf)
            old = mx[n, rows]
            m = jnp.maximum(old, jnp.max(s, -1, keepdims=True))
            p = jnp.exp2(s - m[:, 0:1])
            alpha = jnp.exp2(old - m)
            mx[n, rows] = m
            dn[n, rows] = dn[n, rows] * alpha + jnp.sum(p, -1, keepdims=True)
            acc[n, rows] = acc[n, rows] * alpha + jnp.dot(
                p.astype(BF), v, preferred_element_type=F32
            )
            return 0

        lax.fori_loop(*heads, body, 0)

    def attend_slots(*slots):
        attend([sk.at[k] for k in slots], [sv.at[k] for k in slots])

    def first():
        each(c_img, "wait")
        each(qf_opp, "wait_recv")
        lax.fori_loop(0, NH, first_block, 0)

    def attend_text(*slots):
        n = len(slots) * 64
        at = lax.broadcasted_iota(jnp.int32, (1, n), 1)
        slot = jnp.full((1, n), slots[0], jnp.int32)
        for k in range(1, len(slots)):
            slot = jnp.where(at >= k * 64, slots[k], slot)
        position = at_z(slot) * 64 + jnp.where((at // 32) % 2 == 0, h, 1 - h) * 32 + at % 32
        attend([tk.at[k] for k in slots], [tv.at[k] for k in slots], position < len_ref[0])

    ops = {
        "wf": lambda: each(ws, "finish"),
        "wp": lambda: each(ws, "pass_on"),
        "ws": lambda: each(ws, "start"),
        "wm": lambda: (each(c_cw, "wait"), each(ws, "middle")),
        "ks": lambda: each(ks, "start"),
        "km": lambda: each(ks, "middle"),
        "kp": lambda: each(ks, "pass_on"),
        "kf": lambda: each(ks, "finish"),
        "ms": m_c.start,
        "so": lambda: each(s_opp, "start"),
        "qf": lambda: each(qf_opp, "start"),
        "T1": context,
        "NO": norm,
        "T2": partial_kv,
        "rf": sum_end,
        "to": ring_opposite,
        "P": lambda: pump(1),
        "PP": lambda: pump(2),
        "PA": lambda: pump(16),
        "sf": lambda: each(stale, "finish"),
        "A0": first,
        "ts": lambda: each(text, "start"),
        "tf": lambda: each(text, "finish"),
        "af": lambda: each(tring, "finish"),
    }
    for n in range(4):
        ops[f"r{n}"] = functools.partial(sum_step, n)
        ops[f"t{n}"] = functools.partial(each, text, "forward", n)
        ops[f"a{n}"] = functools.partial(each, tring, "forward", n)
        ops[f"b{n}"] = functools.partial(each, tring[0:2], "forward", n)
        ops[f"c{n}"] = functools.partial(each, tring[2:4], "forward", n)
    for op in PLAN:
        if op in ops:
            ops[op]()
        elif op[0] == "S":
            attend_slots(*map(int, op[1:]))
        else:
            attend_text(*map(int, op[1:]))

    o_c = [net.copy(ob.at[p], ob_in.at[p], opposite) for p in (0, 1)]
    last = [sk.at[4]], [sv.at[4]]
    for p in (0, 1):
        attend(*last, block=1, heads=(3 * p, 3 * p + 3))
        for n in range(3):
            part = acc[3 * p + n, 128:256] / dn[3 * p + n, 128:256]
            ob[p, :, n * HEAD : (n + 1) * HEAD] = part.astype(BF)
        o_c[p].start()
    attend(*last, block=0)
    for n in range(NH):
        out_ref[0, :, head(h * NH + n)] = (acc[n, 0:128] / dn[n, 0:128]).astype(BF)
    for p in (0, 1):
        o_c[p].wait_recv()
        at = pl.multiple_of(theirs + p * HALF // 2, 128)
        out_ref[0, :, pl.ds(at, HALF // 2)] = ob_in[p]
    net.drain()


N_COPIES = 192
PLAN = (
    "ts", "ws", "ms", "ks", "wm", "so", "t1", "t2", "P", "P", "wp", "km",
    "t3", "P", "wf", "tf", "P", "T1", "kp", "qf", "P", "P", "NO", "kf",
    "T2", "r0", "P", "r1", "P", "A0", "r2", "P", "r3", "P", "rf", "P",
    "to", "S17", "a1", "P", "X017", "a2", "P", "S26", "X26", "a3", "P", "X35",
    "PA", "S35", "af", "X4", "sf",
)


def per_device(img_q, fresh_kv, stale_kv, text_states, ctx_weight, kv_weight, modulation, lengths):
    hbm = pl.BlockSpec(memory_space=pltpu.HBM)
    vmem = pl.BlockSpec(memory_space=pltpu.VMEM)
    smem = pl.BlockSpec(memory_space=pltpu.SMEM)
    return pl.pallas_call(
        kernel,
        out_shape=jax.ShapeDtypeStruct((1, 128, 1536), BF),
        in_specs=[hbm] * 7 + [smem],
        out_specs=vmem,
        scratch_shapes=[
            pltpu.VMEM((2, NZ, 32, 2048), BF),
            pltpu.VMEM((192, 192), BF),
            pltpu.VMEM((288, 128), BF),
            pltpu.VMEM((NX, 2, NY, 96, 256), BF),
            pltpu.VMEM((NY, 2, NX, 96, 256), BF),
            pltpu.VMEM((NX, 2, NY, 144, 128), BF),
            pltpu.VMEM((NY, 2, NX, 144, 128), BF),
            pltpu.VMEM((2, 192), F32),
            pltpu.VMEM((2, 8, 256), F32),
            pltpu.VMEM((NZ, 8, 256), F32),
            pltpu.VMEM((NZ, 32, D), F32),
            pltpu.VMEM((2, 4, 2, 32, D // 2), BF),
            pltpu.VMEM((2, 4, 2, 32, D // 2), BF),
            pltpu.VMEM((2, 32, D // 2), BF),
            pltpu.VMEM((NZ, 2, 32, HALF), BF),
            pltpu.VMEM((NZ, 2, 32, HALF), BF),
            pltpu.VMEM((NZ, 2, 128, HALF), BF),
            pltpu.VMEM((NZ, 2, 128, HALF), BF),
            pltpu.VMEM((2, 128, HALF), BF),
            pltpu.VMEM((2, 128, HALF), BF),
            pltpu.VMEM((2, 128, HALF), BF),
            pltpu.VMEM((NH, 256, HEAD), F32),
            pltpu.VMEM((NH, 256, HEAD), F32),
            pltpu.VMEM((NH, 256, HEAD), F32),
            pltpu.VMEM((2, 128, HALF // 2), BF),
            pltpu.VMEM((2, 128, HALF // 2), BF),
            pltpu.SemaphoreType.DMA((N_COPIES,)),
            pltpu.SemaphoreType.DMA((N_COPIES,)),
            pltpu.SemaphoreType.DMA((16,)),
        ],
        compiler_params=pltpu.CompilerParams(
            collective_id=0, has_side_effects=True, vmem_limit_bytes=60 << 20
        ),
    )(img_q, fresh_kv, stale_kv, text_states, ctx_weight.T, kv_weight, modulation, lengths)


def solution(mesh):
    in_specs = (
        P("img", "patch", None),
        P("img", "patch", None),
        P("img", "patch", None),
        P("img", "patch", None),
        P("img", "patch"),
        P("img", "patch"),
        P("img", None, "patch"),
        P("img"),
    )
    return jax.shard_map(
        per_device,
        mesh=mesh,
        in_specs=in_specs,
        out_specs=P("img", "patch", None),
        check_vma=False,
    )
```

```python
import functools
import math

import jax
import jax.numpy as jnp
from jax import lax
from jax.experimental import pallas as pl
from jax.experimental.pallas import tpu as pltpu
from jax.sharding import PartitionSpec as P

D = 3072
HEAD = 128
NX, NY, NZ = 4, 4, 8
HALF = 768
GROUP = 384
NH = 6
MESH = pl.DeviceIdType.MESH
BF = jnp.bfloat16
F32 = jnp.float32


def device(x, y, z, core):
    return ((x * 2 + y % 2) * 2 + core, z * 2 + y // 2)


class Net:
    def __init__(self, send, recv):
        self.send, self.recv, self.used, self.copies = send, recv, 0, []

    def copy(self, src, dst, to):
        n = self.used
        self.used += 1
        c = pltpu.make_async_remote_copy(
            src_ref=src,
            dst_ref=dst,
            send_sem=self.send.at[n],
            recv_sem=self.recv.at[n],
            device_id=to,
            device_id_type=MESH,
        )
        self.copies.append(c)
        return c

    def drain(self):
        for c in self.copies:
            c.wait_send()


class Ring:
    def __init__(self, net, slot, far, left, right, first=None, by_origin=False):
        self.step = {}
        for s in range(4):
            for way in (far, 1 - far):
                if s == 3 and way != far:
                    continue
                a, b, to = (s, s + 1, right) if way == 0 else ((8 - s) % 8, 7 - s, left)
                src, dst = slot(a), slot(a if by_origin else b)
                if s == 0 and first is not None:
                    src = first
                self.step[s, way] = net.copy(src, dst, to)

    def start(self):
        for way in (0, 1):
            self.step[0, way].start()

    def forward(self, s):
        for way in (0, 1):
            self.step[s - 1, way].wait_recv()
            if (s, way) in self.step:
                self.step[s, way].start()

    def finish(self):
        for way in (0, 1):
            if (3, way) in self.step:
                self.step[3, way].wait_recv()


def kernel(
    q_hbm, fresh_hbm, stale_hbm, text_hbm, cw_hbm, kw_hbm, mod_hbm, len_ref, out_hbm,
    tx, kraw, kpack, w0, w1, k0, k1, mraw, mb, st, pt, rs_out, rs_in, tkv, tk, tv, sk, sv, qb, fk, fv,
    acc, mx, dn, ob, send_sem, recv_sem, loc_sem,
):
    img, patch = lax.axis_index("img"), lax.axis_index("patch")
    x, core = img // 4, img % 2
    z, h = patch // 2, patch % 2
    y = h * 2 + (img // 2) % 2
    right, left = device(x, y, (z + 1) % NZ, core), device(x, y, (z + 7) % NZ, core)
    zs = {k: device(x, y, (z + k) % NZ, core) for k in range(1, NZ)}
    xs = {k: device((x + k) % NX, y, z, core) for k in range(1, NX)}
    ys = {k: device(x, (y + k) % NY, z, core) for k in range(1, NY)}
    other = device(x, y, z, 1 - core)
    opposite = ys[2]
    mine, theirs = h * HALF, (1 - h) * HALF
    net = Net(send_sem, recv_sem)

    barrier = pltpu.get_barrier_semaphore()
    peers = [right, left, *xs.values(), *ys.values(), other]
    for d in peers:
        pl.semaphore_signal(barrier, inc=1, device_id=d, device_id_type=MESH)

    def at_z(k):
        return (z + NZ - k) % NZ

    def cols(ref, at, width=HALF):
        return ref.at[0, :, pl.ds(pl.multiple_of(at, 128), width)]

    def group(at, g, value):
        return cols(stale_hbm, (D // 2 if value else 0) + at + g * GROUP, GROUP)

    locals_ = []

    def local(src, dst):
        c = pltpu.make_async_copy(src, dst, loc_sem.at[len(locals_)])
        locals_.append(c)
        c.start()
        return c

    def text_cols(p):
        return text_hbm.at[0, :, pl.ds(p * 2048, 2048)]

    c_kw = local(kw_hbm, kraw)
    c_mod = local(mod_hbm.at[0], mraw)
    cw = [cw_hbm.at[pl.ds(p * 96, 96)] for p in (0, 1)]
    c_cw = [local(cw[0], w0.at[x, core, y]), local(cw[1], w1.at[y, core, x])]
    c_text = [local(text_cols(p), tx.at[p, z]) for p in (0, 1)]
    c_img = [
        local(cols(q_hbm, mine), qb.at[0]),
        local(cols(fresh_hbm, mine), fk.at[0]),
        local(cols(fresh_hbm, D // 2 + mine), fv.at[0]),
        *(local(group(mine, g, 0), sk.at[g, 0, 0]) for g in (0, 1)),
        *(local(group(mine, g, 1), sv.at[g, 0, 0]) for g in (0, 1)),
    ]
    c_kw.wait()
    w = kraw[...]
    kpack[0:192] = w[:, 0:128]
    kpack[192:288] = jnp.concatenate([w[0:96, 128:192], w[96:192, 128:192]], axis=1)
    k0[x, core, y] = kpack[0:144]
    k1[y, core, x] = kpack[144:288]
    c_mod.wait()
    mb[h, 0:2, 0:192] = mraw[...]
    pl.semaphore_wait(barrier, len(peers))

    text = [Ring(net, lambda k, p=p: tx.at[p, at_z(k)], p, left, right, text_cols(p), True) for p in (0, 1)]

    class Spread:
        def __init__(self, buf, i, j, own, first, second):
            self.first = {k: net.copy(own, buf.at[i, core, j], first[k]) for k in first}
            self.second = {k: net.copy(buf.at[i, core], buf.at[i, core], second[k]) for k in second}
            self.core = {k: net.copy(buf.at[(i + 4 - k) % 4, core], buf.at[(i + 4 - k) % 4, core], other) for k in range(4)}

        def start(self):
            for c in self.first.values():
                c.start()

        def middle(self):
            for c in self.first.values():
                c.wait_recv()
            for k in (2, 1, 3):
                self.second[k].start()
            self.core[0].start()

        def pass_on(self):
            for k in (1, 3, 2):
                self.second[k].wait_recv()
                self.core[k].start()

        def finish(self):
            for c in self.core.values():
                c.wait_recv()

    ws = [Spread(w0, x, y, cw[0], ys, xs), Spread(w1, y, x, cw[1], xs, ys)]
    ks = [
        Spread(k0, x, y, kpack.at[pl.ds(0, 144)], ys, xs),
        Spread(k1, y, x, kpack.at[pl.ds(144, 144)], xs, ys),
    ]
    m_c = net.copy(mb.at[h], mb.at[h], opposite)
    s_opp = {
        (g, v): net.copy(group(theirs, g, v), b.at[g, 0, 1], opposite)
        for g in (0, 1)
        for v, b in ((0, sk), (1, sv))
    }
    qf_opp = [
        net.copy(cols(q_hbm, theirs), qb.at[1], opposite),
        net.copy(cols(fresh_hbm, theirs), fk.at[1], opposite),
        net.copy(cols(fresh_hbm, D // 2 + theirs), fv.at[1], opposite),
    ]
    stale = {
        (r, g, v): Ring(
            net, lambda k, b=b, r=r, g=g: b.at[g, k, r], v, left, right,
            None if r else group(mine, g, v),
        )
        for r in (0, 1)
        for g in (0, 1)
        for v, b in ((0, sk), (1, sv))
    }
    stale_work = list(STALE)

    def pump(n):
        for _ in range(n):
            s, r, g = stale_work.pop(0)
            for v in (0, 1):
                if s > 0:
                    stale[r, g, v].forward(s)
                else:
                    if r == 1:
                        s_opp[g, v].wait_recv()
                    stale[r, g, v].start()

    def each(things, method, *args):
        for t in things:
            getattr(t, method)(*args)

    def tile(a, b, i, c, lo):
        return [jnp.concatenate([a[i, c, t], b[t, c, i]], axis=0) for t in (lo, 2 + lo)]

    held = {}

    def context():
        each(c_text, "wait")
        ctx = jnp.zeros((256, 384), F32)
        for i in range(NX):
            blocks = []
            for lo in (0, 1):
                for c in (0, 1):
                    a, b = tile(w0, w1, i, c, lo)
                    blocks.append(jnp.concatenate([a[0:128], b[0:128], a[128:], b[128:]], axis=0))
            rhs = jnp.concatenate(blocks, axis=1)
            lhs = tx[i // 2, :, :, (i % 2) * 1024 : (i % 2 + 1) * 1024].reshape(256, 1024)
            ctx = ctx + lax.dot_general(
                lhs, rhs, (((1,), (1,)), ((), ())), preferred_element_type=F32
            )
        lane = lax.broadcasted_iota(jnp.int32, (256, 128), 1)
        s1 = jnp.sum(ctx, -1, keepdims=True)
        s2 = jnp.sum(ctx * ctx, -1, keepdims=True)
        both = jnp.where(lane == 0, s1, jnp.where(lane == 1, s2, 0.0))
        st[0] = jnp.transpose(both)[0:8]
        st_c = [net.copy(st.at[0], st.at[k], zs[k]) for k in zs]
        for c in st_c:
            c.start()
        held.update(ctx=ctx, st_c=st_c)

    def norm():
        ctx, st_c = held["ctx"], held["st_c"]
        m_c.wait_recv()
        low = lax.broadcasted_iota(jnp.int32, (8, 128), 1) < 64
        ma, mb_ = mb[0], mb[1]
        tail = jnp.where(low, ma[:, 128:256], pltpu.roll(mb_[:, 128:256], 64, 1))
        modul = jnp.concatenate([ma[:, 0:128], mb_[:, 0:128], tail], axis=1)
        for c in st_c:
            c.wait_recv()
        tot = st[0]
        for k in range(1, NZ):
            tot = tot + st[k]
        tot = jnp.transpose(jnp.concatenate([tot, jnp.zeros((120, 256), F32)], axis=0))
        average = tot[:, 0:1] / D
        variance = tot[:, 1:2] / D - average * average
        normed = (
            (ctx - average) * lax.rsqrt(variance + 1e-06) * (1.0 + modul[0:1]) + modul[1:2]
        ).astype(BF)
        held["normed"] = normed

    def partial_kv():
        normed = held["normed"]
        for i in range(NX):
            for lo in (0, 1):
                blocks = []
                for c in (0, 1):
                    a, b = tile(k0, k1, i, c, lo)
                    ra, rb = a[192:], b[192:]
                    last = jnp.concatenate(
                        [
                            jnp.concatenate([ra[:, 0:64], rb[:, 0:64]], axis=1),
                            jnp.concatenate([ra[:, 64:], rb[:, 64:]], axis=1),
                        ],
                        axis=0,
                    )
                    blocks.append(jnp.concatenate([a[0:192], b[0:192], last], axis=1))
                part = lax.dot_general(
                    normed,
                    jnp.concatenate(blocks, axis=0),
                    (((1,), (1,)), ((), ())),
                    preferred_element_type=F32,
                )
                at = (i * 2 + lo) * 384
                pt[:, :, at : at + 384] = part.reshape(NZ, 32, 384)

    parts = (slice(0, D // 2), slice(D // 2, D))
    steps = {}
    for n in range(4):
        for way in (0, 1):
            for p in (way, 1 - way):
                if n > 0 or p == way:
                    to = left if way == 0 else right
                    steps[n, way, p] = net.copy(rs_out.at[way, n, p], rs_in.at[way, n, p], to)

    def sum_step(n):
        for p in (0, 1):
            for way in (0, 1):
                if (n, way, p) not in steps:
                    continue
                term = pt[at_z(4 - n if way == 0 else 4 + n), :, parts[p]]
                if (n - 1, way, p) in steps:
                    steps[n - 1, way, p].wait_recv()
                    term = term + rs_in[way, n - 1, p]
                rs_out[way, n, p] = term.astype(BF)
                steps[n, way, p].start()

    tring = [
        Ring(net, lambda k, b=b, r=r: b.at[k, r], far, left, right)
        for r in (0, 1)
        for far, b in ((0, tk), (1, tv))
    ]
    t_opp = []

    def sum_end():
        for p, b in ((0, tk), (1, tv)):
            for way in (0, 1):
                steps[3, way, p].wait_recv()
            tkv[p] = (pt[z, :, parts[p]] + rs_in[0, 3, p] + rs_in[1, 3, p]).astype(BF)
            c = net.copy(tkv.at[p, :, pl.ds(pl.multiple_of(theirs, 128), HALF)], b.at[0, 1], opposite)
            c.start()
            t_opp.append(c)
            b[0, 0] = tkv[p, :, pl.ds(pl.multiple_of(mine, 128), HALF)]
            tring[p].start()

    def ring_opposite():
        for p in (0, 1):
            t_opp[p].wait_recv()
            tring[2 + p].start()

    c2 = math.log2(math.e) / math.sqrt(HEAD)
    contract = (((1,), (1,)), ((), ()))

    def head(n):
        return pl.ds(n * HEAD, HEAD)

    def scores(q, k):
        return lax.dot_general(q, k, contract, preferred_element_type=F32) * c2

    def first_block(g, n):
        for r in (0, 1):
            at = head(n - 3 * g)
            k = jnp.concatenate([fk[r, :, head(n)], sk[g, 0, 1 - r, :, at]], axis=0)
            v = jnp.concatenate([fv[r, :, head(n)], sv[g, 0, 1 - r, :, at]], axis=0)
            s = scores(qb[r, :, head(n)], k)
            m = jnp.max(s, -1, keepdims=True)
            p = jnp.exp2(s - m)
            rows = pl.ds(r * 128, 128)
            mx[n, rows] = jnp.broadcast_to(m, (128, 128))
            dn[n, rows] = jnp.broadcast_to(jnp.sum(p, -1, keepdims=True), (128, 128))
            acc[n, rows] = jnp.dot(p.astype(BF), v, preferred_element_type=F32)

    def attend(keys, values, mask=None, block=None, heads=(0, NH)):
        first = heads[0]
        rows = slice(None) if block is None else pl.ds(block * 128, 128)

        def body(n):
            if block is None:
                q = qb[:, :, head(n)].reshape(256, HEAD)
            else:
                q = qb[block, :, head(n)]
            k = jnp.concatenate([b[..., head(n - first)].reshape(-1, HEAD) for b in keys], axis=0)
            v = jnp.concatenate([b[..., head(n - first)].reshape(-1, HEAD) for b in values], axis=0)
            s = scores(q, k)
            if mask is not None:
                s = jnp.where(mask, s, -jnp.inf)
            old = mx[n, rows]
            m = jnp.maximum(old, jnp.max(s, -1, keepdims=True))
            p = jnp.exp2(s - m[:, 0:1])
            alpha = jnp.exp2(old - m)
            mx[n, rows] = m
            dn[n, rows] = dn[n, rows] * alpha + jnp.sum(p, -1, keepdims=True)
            acc[n, rows] = acc[n, rows] * alpha + jnp.dot(
                p.astype(BF), v, preferred_element_type=F32
            )

        for n in range(*heads):
            body(n)

    def attend_slots(g, *slots, block=None):
        attend(
            [sk.at[g, k] for k in slots],
            [sv.at[g, k] for k in slots],
            block=block,
            heads=(3 * g, 3 * g + 3),
        )

    def first():
        each(c_img, "wait")
        each(qf_opp, "wait_recv")
        for g in (0, 1):
            for n in range(3 * g, 3 * g + 3):
                first_block(g, n)

    def attend_text(*slots):
        n = len(slots) * 64
        at = lax.broadcasted_iota(jnp.int32, (1, n), 1)
        slot = jnp.full((1, n), slots[0], jnp.int32)
        for k in range(1, len(slots)):
            slot = jnp.where(at >= k * 64, slots[k], slot)
        position = at_z(slot) * 64 + jnp.where((at // 32) % 2 == 0, h, 1 - h) * 32 + at % 32
        attend([tk.at[k] for k in slots], [tv.at[k] for k in slots], position < len_ref[0])

    def out_cols(g):
        return cols(out_hbm, mine + g * GROUP, GROUP)

    o_c = [net.copy(ob.at[1, g], out_cols(g), opposite) for g in (0, 1)]
    own = []

    def finish(g):
        for r in (0, 1):
            for v in (0, 1):
                stale[r, g, v].finish()
        for block in (1, 0):
            attend_slots(g, 4, block=block)
            rows = pl.ds(block * 128, 128)
            for n in range(3):
                part = acc[3 * g + n, rows] / dn[3 * g + n, rows]
                ob[block, g, :, n * HEAD : (n + 1) * HEAD] = part.astype(BF)
            if block == 1:
                o_c[g].start()
            else:
                own.append(local(ob.at[0, g], out_cols(g)))

    ops = {
        "wf": lambda: each(ws, "finish"),
        "wp": lambda: each(ws, "pass_on"),
        "ws": lambda: each(ws, "start"),
        "wm": lambda: (each(c_cw, "wait"), each(ws, "middle")),
        "ks": lambda: each(ks, "start"),
        "km": lambda: each(ks, "middle"),
        "kp": lambda: each(ks, "pass_on"),
        "kf": lambda: each(ks, "finish"),
        "ms": m_c.start,
        "so": lambda: each(s_opp.values(), "start"),
        "qf": lambda: each(qf_opp, "start"),
        "T1": context,
        "NO": norm,
        "T2": partial_kv,
        "rf": sum_end,
        "to": ring_opposite,
        "P": lambda: pump(1),
        "PA": lambda: pump(len(stale_work)),
        "F0": lambda: finish(0),
        "F1": lambda: finish(1),
        "A0": first,
        "ts": lambda: each(text, "start"),
        "tf": lambda: each(text, "finish"),
        "af": lambda: each(tring, "finish"),
    }
    for n in range(4):
        ops[f"r{n}"] = functools.partial(sum_step, n)
        ops[f"t{n}"] = functools.partial(each, text, "forward", n)
        ops[f"a{n}"] = functools.partial(each, tring, "forward", n)
        ops[f"b{n}"] = functools.partial(each, tring[0:2], "forward", n)
        ops[f"c{n}"] = functools.partial(each, tring[2:4], "forward", n)
    for op in PLAN:
        if op in ops:
            ops[op]()
        elif op[0] == "S":
            attend_slots(0, *map(int, op[1:]))
            attend_slots(1, *map(int, op[1:]))
        elif op[0] in "DE":
            attend_slots("DE".index(op[0]), *map(int, op[1:]))
        else:
            attend_text(*map(int, op[1:]))

    each(own, "wait")
    each(o_c, "wait_recv")
    net.drain()


N_COPIES = 224
STALE = (
    *((0, r, g) for r in (0, 1) for g in (0, 1)),
    *((s, r, g) for s in (1, 2, 3) for g in (0, 1) for r in (0, 1)),
)
PLAN = (
    "ts", "ws", "ms", "wm", "ks", "so", "t1", "t2", "P", "P", "t3", "wp",
    "km", "P", "P", "wf", "tf", "T1", "kp", "qf", "P", "P", "NO", "kf",
    "T2", "r0", "P", "r1", "P", "A0", "r2", "P", "r3", "P", "rf", "P",
    "to", "S17", "a1", "P", "X017", "a2", "P", "S26", "X26", "a3", "P", "PA",
    "S35", "af", "X354", "F0", "F1",
)


def per_device(img_q, fresh_kv, stale_kv, text_states, ctx_weight, kv_weight, modulation, lengths):
    hbm = pl.BlockSpec(memory_space=pltpu.HBM)
    smem = pl.BlockSpec(memory_space=pltpu.SMEM)
    return pl.pallas_call(
        kernel,
        out_shape=jax.ShapeDtypeStruct((1, 128, 1536), BF),
        in_specs=[hbm] * 7 + [smem],
        out_specs=hbm,
        scratch_shapes=[
            pltpu.VMEM((2, NZ, 32, 2048), BF),
            pltpu.VMEM((192, 192), BF),
            pltpu.VMEM((288, 128), BF),
            pltpu.VMEM((NX, 2, NY, 96, 256), BF),
            pltpu.VMEM((NY, 2, NX, 96, 256), BF),
            pltpu.VMEM((NX, 2, NY, 144, 128), BF),
            pltpu.VMEM((NY, 2, NX, 144, 128), BF),
            pltpu.VMEM((2, 192), F32),
            pltpu.VMEM((2, 8, 256), F32),
            pltpu.VMEM((NZ, 8, 256), F32),
            pltpu.VMEM((NZ, 32, D), F32),
            pltpu.VMEM((2, 4, 2, 32, D // 2), BF),
            pltpu.VMEM((2, 4, 2, 32, D // 2), BF),
            pltpu.VMEM((2, 32, D // 2), BF),
            pltpu.VMEM((NZ, 2, 32, HALF), BF),
            pltpu.VMEM((NZ, 2, 32, HALF), BF),
            pltpu.VMEM((2, NZ, 2, 128, GROUP), BF),
            pltpu.VMEM((2, NZ, 2, 128, GROUP), BF),
            pltpu.VMEM((2, 128, HALF), BF),
            pltpu.VMEM((2, 128, HALF), BF),
            pltpu.VMEM((2, 128, HALF), BF),
            pltpu.VMEM((NH, 256, HEAD), F32),
            pltpu.VMEM((NH, 256, HEAD), F32),
            pltpu.VMEM((NH, 256, HEAD), F32),
            pltpu.VMEM((2, 2, 128, HALF // 2), BF),
            pltpu.SemaphoreType.DMA((N_COPIES,)),
            pltpu.SemaphoreType.DMA((N_COPIES,)),
            pltpu.SemaphoreType.DMA((24,)),
        ],
        compiler_params=pltpu.CompilerParams(
            collective_id=0, has_side_effects=True, vmem_limit_bytes=58 << 20
        ),
    )(img_q, fresh_kv, stale_kv, text_states, ctx_weight.T, kv_weight, modulation, lengths)


def solution(mesh):
    in_specs = (
        P("img", "patch", None),
        P("img", "patch", None),
        P("img", "patch", None),
        P("img", "patch", None),
        P("img", "patch"),
        P("img", "patch"),
        P("img", None, "patch"),
        P("img"),
    )
    return jax.shard_map(
        per_device,
        mesh=mesh,
        in_specs=in_specs,
        out_specs=P("img", "patch", None),
        check_vma=False,
    )
```

```python
import functools
import math

import jax
import jax.numpy as jnp
from jax import lax
from jax.experimental import pallas as pl
from jax.experimental.pallas import tpu as pltpu
from jax.sharding import PartitionSpec as P

D = 3072
HEAD = 128
NX, NY, NZ = 4, 4, 8
HALF = 768
GROUP = 384
NH = 6
MESH = pl.DeviceIdType.MESH
BF = jnp.bfloat16
F32 = jnp.float32


def device(x, y, z, core):
    return ((x * 2 + y % 2) * 2 + core, z * 2 + y // 2)


class Net:
    def __init__(self, send, recv):
        self.send, self.recv, self.used, self.copies = send, recv, 0, []

    def copy(self, src, dst, to):
        n = self.used
        self.used += 1
        c = pltpu.make_async_remote_copy(
            src_ref=src,
            dst_ref=dst,
            send_sem=self.send.at[n],
            recv_sem=self.recv.at[n],
            device_id=to,
            device_id_type=MESH,
        )
        self.copies.append(c)
        return c

    def drain(self):
        for c in self.copies:
            c.wait_send()


class Ring:
    def __init__(self, net, slot, far, left, right, first=None, by_origin=False):
        self.step = {}
        for s in range(4):
            for way in (far, 1 - far):
                if s == 3 and way != far:
                    continue
                a, b, to = (s, s + 1, right) if way == 0 else ((8 - s) % 8, 7 - s, left)
                src, dst = slot(a), slot(a if by_origin else b)
                if s == 0 and first is not None:
                    src = first
                self.step[s, way] = net.copy(src, dst, to)

    def start(self):
        for way in (0, 1):
            self.step[0, way].start()

    def forward(self, s):
        for way in (0, 1):
            self.step[s - 1, way].wait_recv()
            if (s, way) in self.step:
                self.step[s, way].start()

    def finish(self):
        for way in (0, 1):
            if (3, way) in self.step:
                self.step[3, way].wait_recv()


def kernel(
    q_hbm, fresh_hbm, stale_hbm, text_hbm, cw_hbm, kw_hbm, mod_hbm, len_ref, out_hbm,
    tx, kraw, kpack, w0, w1, k0, k1, mraw, mb, st, pt, rs_out, rs_in, tkv, tk, tv, sk, sv, qb, fk, fv,
    acc, mx, dn, ob, send_sem, recv_sem, loc_sem,
):
    img, patch = lax.axis_index("img"), lax.axis_index("patch")
    x, core = img // 4, img % 2
    z, h = patch // 2, patch % 2
    y = h * 2 + (img // 2) % 2
    right, left = device(x, y, (z + 1) % NZ, core), device(x, y, (z + 7) % NZ, core)
    zs = {k: device(x, y, (z + k) % NZ, core) for k in range(1, NZ)}
    xs = {k: device((x + k) % NX, y, z, core) for k in range(1, NX)}
    ys = {k: device(x, (y + k) % NY, z, core) for k in range(1, NY)}
    other = device(x, y, z, 1 - core)
    opposite = ys[2]
    mine, theirs = h * HALF, (1 - h) * HALF
    net = Net(send_sem, recv_sem)

    barrier = pltpu.get_barrier_semaphore()
    peers = [right, left, *xs.values(), *ys.values(), other]
    for d in peers:
        pl.semaphore_signal(barrier, inc=1, device_id=d, device_id_type=MESH)

    def at_z(k):
        return (z + NZ - k) % NZ

    def cols(ref, at, width=HALF):
        return ref.at[0, :, pl.ds(pl.multiple_of(at, 128), width)]

    def group(at, g, value):
        return cols(stale_hbm, (D // 2 if value else 0) + at + g * GROUP, GROUP)

    locals_ = []

    def local(src, dst):
        c = pltpu.make_async_copy(src, dst, loc_sem.at[len(locals_)])
        locals_.append(c)
        c.start()
        return c

    def text_cols(p):
        return text_hbm.at[0, :, pl.ds(p * 1024, 1024)]

    c_kw = local(kw_hbm, kraw)
    c_mod = local(mod_hbm.at[0], mraw)
    cw = [cw_hbm.at[pl.ds(p * 96, 96)] for p in (0, 1)]
    c_cw = [local(cw[0], w0.at[x, core, y]), local(cw[1], w1.at[y, core, x])]
    c_text = [local(text_cols(p), tx.at[p, z]) for p in range(4)]
    c_img = [
        local(cols(q_hbm, mine), qb.at[0]),
        local(cols(fresh_hbm, mine), fk.at[0]),
        local(cols(fresh_hbm, D // 2 + mine), fv.at[0]),
        *(local(group(mine, g, 0), sk.at[g, 0, 0]) for g in (0, 1)),
        *(local(group(mine, g, 1), sv.at[g, 0, 0]) for g in (0, 1)),
    ]
    c_kw.wait()
    w = kraw[...]
    kpack[0:192] = w[:, 0:128]
    kpack[192:288] = jnp.concatenate([w[0:96, 128:192], w[96:192, 128:192]], axis=1)
    k0[x, core, y] = kpack[0:144]
    k1[y, core, x] = kpack[144:288]
    c_mod.wait()
    mb[h, 0:2, 0:192] = mraw[...]
    pl.semaphore_wait(barrier, len(peers))

    text = [
        Ring(net, lambda k, p=p: tx.at[p, at_z(k)], p % 2, left, right, text_cols(p), True)
        for p in range(4)
    ]

    class Spread:
        def __init__(self, buf, i, j, own, first, second):
            self.first = {k: net.copy(own, buf.at[i, core, j], first[k]) for k in first}
            self.second = {k: net.copy(buf.at[i, core], buf.at[i, core], second[k]) for k in second}
            self.core = {k: net.copy(buf.at[(i + 4 - k) % 4, core], buf.at[(i + 4 - k) % 4, core], other) for k in range(4)}

        def start(self):
            for c in self.first.values():
                c.start()

        def middle(self):
            for c in self.first.values():
                c.wait_recv()
            for k in (2, 1, 3):
                self.second[k].start()
            self.core[0].start()

        def pass_on(self):
            for k in (1, 3, 2):
                self.second[k].wait_recv()
                self.core[k].start()

        def finish(self):
            for c in self.core.values():
                c.wait_recv()

    ws = [Spread(w0, x, y, cw[0], ys, xs), Spread(w1, y, x, cw[1], xs, ys)]
    ks = [
        Spread(k0, x, y, kpack.at[pl.ds(0, 144)], ys, xs),
        Spread(k1, y, x, kpack.at[pl.ds(144, 144)], xs, ys),
    ]
    m_c = net.copy(mb.at[h], mb.at[h], opposite)
    s_opp = {
        (g, v): net.copy(group(theirs, g, v), b.at[g, 0, 1], opposite)
        for g in (0, 1)
        for v, b in ((0, sk), (1, sv))
    }
    qf_opp = [
        net.copy(cols(q_hbm, theirs), qb.at[1], opposite),
        net.copy(cols(fresh_hbm, theirs), fk.at[1], opposite),
        net.copy(cols(fresh_hbm, D // 2 + theirs), fv.at[1], opposite),
    ]
    stale = {
        (r, g, v): Ring(
            net, lambda k, b=b, r=r, g=g: b.at[g, k, r], v, left, right,
            None if r else group(mine, g, v),
        )
        for r in (0, 1)
        for g in (0, 1)
        for v, b in ((0, sk), (1, sv))
    }
    stale_work = list(STALE)

    def pump(n):
        for _ in range(n):
            s, r, g = stale_work.pop(0)
            for v in (0, 1):
                if s > 0:
                    stale[r, g, v].forward(s)
                else:
                    if r == 1:
                        s_opp[g, v].wait_recv()
                    stale[r, g, v].start()

    def each(things, method, *args):
        for t in things:
            getattr(t, method)(*args)

    def tile(a, b, i, c, lo):
        return [jnp.concatenate([a[i, c, t], b[t, c, i]], axis=0) for t in (lo, 2 + lo)]

    held = {}

    def context():
        each(c_text, "wait")
        ctx = jnp.zeros((256, 384), F32)
        for i in range(NX):
            blocks = []
            for lo in (0, 1):
                for c in (0, 1):
                    a, b = tile(w0, w1, i, c, lo)
                    blocks.append(jnp.concatenate([a[0:128], b[0:128], a[128:], b[128:]], axis=0))
            rhs = jnp.concatenate(blocks, axis=1)
            text[i].finish()
            lhs = tx[i].reshape(256, 1024)
            ctx = ctx + lax.dot_general(
                lhs, rhs, (((1,), (1,)), ((), ())), preferred_element_type=F32
            )
        lane = lax.broadcasted_iota(jnp.int32, (256, 128), 1)
        s1 = jnp.sum(ctx, -1, keepdims=True)
        s2 = jnp.sum(ctx * ctx, -1, keepdims=True)
        both = jnp.where(lane == 0, s1, jnp.where(lane == 1, s2, 0.0))
        st[0] = jnp.transpose(both)[0:2]
        st_c = [net.copy(st.at[0], st.at[k], zs[k]) for k in zs]
        for c in st_c:
            c.start()
        held.update(ctx=ctx, st_c=st_c)

    def norm():
        ctx, st_c = held["ctx"], held["st_c"]
        m_c.wait_recv()
        low = lax.broadcasted_iota(jnp.int32, (8, 128), 1) < 64
        ma, mb_ = mb[0], mb[1]
        tail = jnp.where(low, ma[:, 128:256], pltpu.roll(mb_[:, 128:256], 64, 1))
        modul = jnp.concatenate([ma[:, 0:128], mb_[:, 0:128], tail], axis=1)
        for c in st_c:
            c.wait_recv()
        tot = st[0]
        for k in range(1, NZ):
            tot = tot + st[k]
        tot = jnp.transpose(jnp.concatenate([tot, jnp.zeros((126, 256), F32)], axis=0))
        average = tot[:, 0:1] / D
        variance = tot[:, 1:2] / D - average * average
        normed = (
            (ctx - average) * lax.rsqrt(variance + 1e-06) * (1.0 + modul[0:1]) + modul[1:2]
        ).astype(BF)
        held["normed"] = normed

    def partial_kv():
        normed = held["normed"]
        for i in range(NX):
            for lo in (0, 1):
                blocks = []
                for c in (0, 1):
                    a, b = tile(k0, k1, i, c, lo)
                    ra, rb = a[192:], b[192:]
                    last = jnp.concatenate(
                        [
                            jnp.concatenate([ra[:, 0:64], rb[:, 0:64]], axis=1),
                            jnp.concatenate([ra[:, 64:], rb[:, 64:]], axis=1),
                        ],
                        axis=0,
                    )
                    blocks.append(jnp.concatenate([a[0:192], b[0:192], last], axis=1))
                part = lax.dot_general(
                    normed,
                    jnp.concatenate(blocks, axis=0),
                    (((1,), (1,)), ((), ())),
                    preferred_element_type=F32,
                )
                at = (i * 2 + lo) * 384
                pt[:, :, at : at + 384] = part.reshape(NZ, 32, 384)

    parts = (slice(0, D // 2), slice(D // 2, D))
    steps = {}
    for n in range(4):
        for way in (0, 1):
            for p in (way, 1 - way):
                if n > 0 or p == way:
                    to = left if way == 0 else right
                    steps[n, way, p] = net.copy(rs_out.at[way, n, p], rs_in.at[way, n, p], to)

    def sum_step(n):
        for p in (0, 1):
            for way in (0, 1):
                if (n, way, p) not in steps:
                    continue
                term = pt[at_z(4 - n if way == 0 else 4 + n), :, parts[p]]
                if (n - 1, way, p) in steps:
                    steps[n - 1, way, p].wait_recv()
                    term = term + rs_in[way, n - 1, p]
                rs_out[way, n, p] = term.astype(BF)
                steps[n, way, p].start()

    tring = [
        Ring(net, lambda k, b=b, r=r: b.at[k, r], far, left, right)
        for r in (0, 1)
        for far, b in ((0, tk), (1, tv))
    ]
    t_opp = []

    def sum_end():
        for p, b in ((0, tk), (1, tv)):
            for way in (0, 1):
                steps[3, way, p].wait_recv()
            tkv[p] = (pt[z, :, parts[p]] + rs_in[0, 3, p] + rs_in[1, 3, p]).astype(BF)
            c = net.copy(tkv.at[p, :, pl.ds(pl.multiple_of(theirs, 128), HALF)], b.at[0, 1], opposite)
            c.start()
            t_opp.append(c)
            b[0, 0] = tkv[p, :, pl.ds(pl.multiple_of(mine, 128), HALF)]
            tring[p].start()

    def ring_opposite():
        for p in (0, 1):
            t_opp[p].wait_recv()
            tring[2 + p].start()

    c2 = math.log2(math.e) / math.sqrt(HEAD)
    contract = (((1,), (1,)), ((), ()))

    def head(n):
        return pl.ds(n * HEAD, HEAD)

    def scores(q, k):
        return lax.dot_general(q, k, contract, preferred_element_type=F32) * c2

    def first_block(g, n):
        for r in (0, 1):
            at = head(n - 3 * g)
            k = jnp.concatenate([fk[r, :, head(n)], sk[g, 0, 1 - r, :, at]], axis=0)
            v = jnp.concatenate([fv[r, :, head(n)], sv[g, 0, 1 - r, :, at]], axis=0)
            s = scores(qb[r, :, head(n)], k)
            m = jnp.max(s, -1, keepdims=True)
            p = jnp.exp2(s - m)
            rows = pl.ds(r * 128, 128)
            mx[n, rows] = jnp.broadcast_to(m, (128, 128))
            dn[n, rows] = jnp.broadcast_to(jnp.sum(p, -1, keepdims=True), (128, 128))
            acc[n, rows] = jnp.dot(p.astype(BF), v, preferred_element_type=F32)

    def attend(keys, values, mask=None, block=None, heads=(0, NH)):
        first = heads[0]
        rows = slice(None) if block is None else pl.ds(block * 128, 128)

        def body(n):
            if block is None:
                q = qb[:, :, head(n)].reshape(256, HEAD)
            else:
                q = qb[block, :, head(n)]
            k = jnp.concatenate([b[..., head(n - first)].reshape(-1, HEAD) for b in keys], axis=0)
            v = jnp.concatenate([b[..., head(n - first)].reshape(-1, HEAD) for b in values], axis=0)
            s = scores(q, k)
            if mask is not None:
                s = jnp.where(mask, s, -jnp.inf)
            old = mx[n, rows]
            m = jnp.maximum(old, jnp.max(s, -1, keepdims=True))
            p = jnp.exp2(s - m[:, 0:1])
            alpha = jnp.exp2(old - m)
            mx[n, rows] = m
            dn[n, rows] = dn[n, rows] * alpha + jnp.sum(p, -1, keepdims=True)
            acc[n, rows] = acc[n, rows] * alpha + jnp.dot(
                p.astype(BF), v, preferred_element_type=F32
            )

        for n in range(*heads):
            body(n)

    def attend_slots(g, *slots, block=None):
        attend(
            [sk.at[g, k] for k in slots],
            [sv.at[g, k] for k in slots],
            block=block,
            heads=(3 * g, 3 * g + 3),
        )

    def first():
        each(c_img, "wait")
        each(qf_opp, "wait_recv")
        for g in (0, 1):
            for n in range(3 * g, 3 * g + 3):
                first_block(g, n)

    def attend_text(*slots):
        n = len(slots) * 64
        at = lax.broadcasted_iota(jnp.int32, (1, n), 1)
        slot = jnp.full((1, n), slots[0], jnp.int32)
        for k in range(1, len(slots)):
            slot = jnp.where(at >= k * 64, slots[k], slot)
        position = at_z(slot) * 64 + jnp.where((at // 32) % 2 == 0, h, 1 - h) * 32 + at % 32
        attend([tk.at[k] for k in slots], [tv.at[k] for k in slots], position < len_ref[0])

    def out_cols(g):
        return cols(out_hbm, mine + g * GROUP, GROUP)

    o_c = [net.copy(ob.at[1, g], out_cols(g), opposite) for g in (0, 1)]
    own = []

    def finish(g):
        for r in (0, 1):
            for v in (0, 1):
                stale[r, g, v].finish()
        for block in (1, 0):
            attend_slots(g, 4, block=block)
            rows = pl.ds(block * 128, 128)
            for n in range(3):
                part = acc[3 * g + n, rows] / dn[3 * g + n, rows]
                ob[block, g, :, n * HEAD : (n + 1) * HEAD] = part.astype(BF)
            if block == 1:
                o_c[g].start()
            else:
                own.append(local(ob.at[0, g], out_cols(g)))

    ops = {
        "wf": lambda: each(ws, "finish"),
        "wp": lambda: each(ws, "pass_on"),
        "ws": lambda: each(ws, "start"),
        "wm": lambda: (each(c_cw, "wait"), each(ws, "middle")),
        "ks": lambda: each(ks, "start"),
        "km": lambda: each(ks, "middle"),
        "kp": lambda: each(ks, "pass_on"),
        "kf": lambda: each(ks, "finish"),
        "ms": m_c.start,
        "so": lambda: each(s_opp.values(), "start"),
        "qf": lambda: each(qf_opp, "start"),
        "T1": context,
        "NO": norm,
        "T2": partial_kv,
        "rf": sum_end,
        "to": ring_opposite,
        "P": lambda: pump(1),
        "PA": lambda: pump(len(stale_work)),
        "F0": lambda: finish(0),
        "F1": lambda: finish(1),
        "A0": first,
        "ts": lambda: each(text, "start"),
        "af": lambda: each(tring, "finish"),
    }
    for n in range(4):
        ops[f"r{n}"] = functools.partial(sum_step, n)
        ops[f"t{n}"] = functools.partial(each, text, "forward", n)
        ops[f"a{n}"] = functools.partial(each, tring, "forward", n)
        ops[f"b{n}"] = functools.partial(each, tring[0:2], "forward", n)
        ops[f"c{n}"] = functools.partial(each, tring[2:4], "forward", n)
    for op in PLAN:
        if op in ops:
            ops[op]()
        elif op[0] == "S":
            attend_slots(0, *map(int, op[1:]))
            attend_slots(1, *map(int, op[1:]))
        elif op[0] in "DE":
            attend_slots("DE".index(op[0]), *map(int, op[1:]))
        else:
            attend_text(*map(int, op[1:]))

    each(own, "wait")
    each(o_c, "wait_recv")
    net.drain()


N_COPIES = 224
STALE = (
    *((0, r, g) for r in (0, 1) for g in (0, 1)),
    *((s, r, g) for s in (1, 2, 3) for g in (0, 1) for r in (0, 1)),
)
PLAN = (
    "ts", "ws", "ms", "wm", "ks", "so", "t1", "t2", "P", "t3", "P", "wp",
    "km", "P", "P", "wf", "T1", "kp", "qf", "P", "P", "NO", "kf", "T2",
    "r0", "P", "r1", "P", "A0", "r2", "P", "r3", "P", "rf", "P", "to",
    "S17", "a1", "P", "X017", "a2", "P", "S26", "X26", "a3", "P", "PA", "S35",
    "af", "X354", "F0", "F1",
)


def per_device(img_q, fresh_kv, stale_kv, text_states, ctx_weight, kv_weight, modulation, lengths):
    hbm = pl.BlockSpec(memory_space=pltpu.HBM)
    smem = pl.BlockSpec(memory_space=pltpu.SMEM)
    return pl.pallas_call(
        kernel,
        out_shape=jax.ShapeDtypeStruct((1, 128, 1536), BF),
        in_specs=[hbm] * 7 + [smem],
        out_specs=hbm,
        scratch_shapes=[
            pltpu.VMEM((4, NZ, 32, 1024), BF),
            pltpu.VMEM((192, 192), BF),
            pltpu.VMEM((288, 128), BF),
            pltpu.VMEM((NX, 2, NY, 96, 256), BF),
            pltpu.VMEM((NY, 2, NX, 96, 256), BF),
            pltpu.VMEM((NX, 2, NY, 144, 128), BF),
            pltpu.VMEM((NY, 2, NX, 144, 128), BF),
            pltpu.VMEM((2, 192), F32),
            pltpu.VMEM((2, 8, 256), F32),
            pltpu.VMEM((NZ, 2, 256), F32),
            pltpu.VMEM((NZ, 32, D), F32),
            pltpu.VMEM((2, 4, 2, 32, D // 2), BF),
            pltpu.VMEM((2, 4, 2, 32, D // 2), BF),
            pltpu.VMEM((2, 32, D // 2), BF),
            pltpu.VMEM((NZ, 2, 32, HALF), BF),
            pltpu.VMEM((NZ, 2, 32, HALF), BF),
            pltpu.VMEM((2, NZ, 2, 128, GROUP), BF),
            pltpu.VMEM((2, NZ, 2, 128, GROUP), BF),
            pltpu.VMEM((2, 128, HALF), BF),
            pltpu.VMEM((2, 128, HALF), BF),
            pltpu.VMEM((2, 128, HALF), BF),
            pltpu.VMEM((NH, 256, HEAD), F32),
            pltpu.VMEM((NH, 256, HEAD), F32),
            pltpu.VMEM((NH, 256, HEAD), F32),
            pltpu.VMEM((2, 2, 128, HALF // 2), BF),
            pltpu.SemaphoreType.DMA((N_COPIES,)),
            pltpu.SemaphoreType.DMA((N_COPIES,)),
            pltpu.SemaphoreType.DMA((24,)),
        ],
        compiler_params=pltpu.CompilerParams(
            collective_id=0, has_side_effects=True, vmem_limit_bytes=58 << 20
        ),
    )(img_q, fresh_kv, stale_kv, text_states, ctx_weight.T, kv_weight, modulation, lengths)


def solution(mesh):
    in_specs = (
        P("img", "patch", None),
        P("img", "patch", None),
        P("img", "patch", None),
        P("img", "patch", None),
        P("img", "patch"),
        P("img", "patch"),
        P("img", None, "patch"),
        P("img"),
    )
    return jax.shard_map(
        per_device,
        mesh=mesh,
        in_specs=in_specs,
        out_specs=P("img", "patch", None),
        check_vma=False,
    )
```

```python
import functools
import math

import jax
import jax.numpy as jnp
from jax import lax
from jax.experimental import pallas as pl
from jax.experimental.pallas import tpu as pltpu
from jax.sharding import PartitionSpec as P

D = 3072
HEAD = 128
NX, NY, NZ = 4, 4, 8
HALF = 768
GROUP = 384
NH = 6
MESH = pl.DeviceIdType.MESH
BF = jnp.bfloat16
F32 = jnp.float32


def device(x, y, z, core):
    return ((x * 2 + y % 2) * 2 + core, z * 2 + y // 2)


class Net:
    def __init__(self, send, recv):
        self.send, self.recv, self.used, self.copies = send, recv, 0, []

    def copy(self, src, dst, to):
        n = self.used
        self.used += 1
        c = pltpu.make_async_remote_copy(
            src_ref=src,
            dst_ref=dst,
            send_sem=self.send.at[n],
            recv_sem=self.recv.at[n],
            device_id=to,
            device_id_type=MESH,
        )
        self.copies.append(c)
        return c

    def drain(self):
        for c in self.copies:
            c.wait_send()


class Ring:
    def __init__(self, net, slot, far, left, right, first=None, by_origin=False):
        self.step = {}
        for s in range(4):
            for way in (far, 1 - far):
                if s == 3 and way != far:
                    continue
                a, b, to = (s, s + 1, right) if way == 0 else ((8 - s) % 8, 7 - s, left)
                src, dst = slot(a), slot(a if by_origin else b)
                if s == 0 and first is not None:
                    src = first
                self.step[s, way] = net.copy(src, dst, to)

    def start(self):
        for way in (0, 1):
            self.step[0, way].start()

    def forward(self, s):
        for way in (0, 1):
            self.step[s - 1, way].wait_recv()
            if (s, way) in self.step:
                self.step[s, way].start()

    def finish(self):
        for way in (0, 1):
            if (3, way) in self.step:
                self.step[3, way].wait_recv()


def kernel(
    q_hbm, fresh_hbm, stale_hbm, text_hbm, cw_hbm, kw_hbm, mod_hbm, len_ref, out_hbm,
    tx, kraw, kpack, w0, w1, k0, k1, mraw, mb, st, pt, rs_out, rs_in, tkv, tk, tv, sk, sv, qb, fk, fv,
    acc, mx, dn, ob, send_sem, recv_sem, loc_sem,
):
    img, patch = lax.axis_index("img"), lax.axis_index("patch")
    x, core = img // 4, img % 2
    z, h = patch // 2, patch % 2
    y = h * 2 + (img // 2) % 2
    right, left = device(x, y, (z + 1) % NZ, core), device(x, y, (z + 7) % NZ, core)
    zs = {k: device(x, y, (z + k) % NZ, core) for k in range(1, NZ)}
    xs = {k: device((x + k) % NX, y, z, core) for k in range(1, NX)}
    ys = {k: device(x, (y + k) % NY, z, core) for k in range(1, NY)}
    other = device(x, y, z, 1 - core)
    opposite = ys[2]
    mine, theirs = h * HALF, (1 - h) * HALF
    net = Net(send_sem, recv_sem)

    barrier = pltpu.get_barrier_semaphore()
    peers = [right, left, *xs.values(), *ys.values(), other]
    for d in peers:
        pl.semaphore_signal(barrier, inc=1, device_id=d, device_id_type=MESH)

    def at_z(k):
        return (z + NZ - k) % NZ

    def cols(ref, at, width=HALF):
        return ref.at[0, :, pl.ds(pl.multiple_of(at, 128), width)]

    def group(at, g, value):
        return cols(stale_hbm, (D // 2 if value else 0) + at + g * GROUP, GROUP)

    locals_ = []

    def local(src, dst):
        c = pltpu.make_async_copy(src, dst, loc_sem.at[len(locals_)])
        locals_.append(c)
        c.start()
        return c

    def text_cols(p):
        return text_hbm.at[0, :, pl.ds(p * 1024, 1024)]

    c_kw = local(kw_hbm, kraw)
    c_mod = local(mod_hbm.at[0], mraw)
    cw = [cw_hbm.at[pl.ds(p * 96, 96)] for p in (0, 1)]
    c_cw = [local(cw[0], w0.at[x, core, y]), local(cw[1], w1.at[y, core, x])]
    c_text = [local(text_cols(p), tx.at[p, z]) for p in range(4)]
    c_img = [
        local(cols(q_hbm, mine), qb.at[0]),
        local(cols(fresh_hbm, mine), fk.at[0]),
        local(cols(fresh_hbm, D // 2 + mine), fv.at[0]),
        *(local(group(mine, g, 0), sk.at[g, 0, 0]) for g in (0, 1)),
        *(local(group(mine, g, 1), sv.at[g, 0, 0]) for g in (0, 1)),
    ]
    c_kw.wait()
    w = kraw[...]
    kpack[0:192] = w[:, 0:128]
    kpack[192:288] = jnp.concatenate([w[0:96, 128:192], w[96:192, 128:192]], axis=1)
    k0[x, core, y] = kpack[0:144]
    k1[y, core, x] = kpack[144:288]
    c_mod.wait()
    mb[h, 0:2, 0:192] = mraw[...]
    for c in (*c_text, *c_img):
        c.wait()
    pl.semaphore_wait(barrier, len(peers))

    text = [
        Ring(net, lambda k, p=p: tx.at[p, at_z(k)], p % 2, left, right, by_origin=True)
        for p in range(4)
    ]

    class Spread:
        def __init__(self, buf, i, j, own, first, second):
            self.first = {k: net.copy(own, buf.at[i, core, j], first[k]) for k in first}
            self.second = {k: net.copy(buf.at[i, core], buf.at[i, core], second[k]) for k in second}
            self.core = {k: net.copy(buf.at[(i + 4 - k) % 4, core], buf.at[(i + 4 - k) % 4, core], other) for k in range(4)}

        def start(self):
            for c in self.first.values():
                c.start()

        def middle(self):
            for c in self.first.values():
                c.wait_recv()
            for k in (2, 1, 3):
                self.second[k].start()
            self.core[0].start()

        def pass_on(self):
            for k in (1, 3, 2):
                self.second[k].wait_recv()
                self.core[k].start()

        def finish(self):
            for c in self.core.values():
                c.wait_recv()

    ws = [Spread(w0, x, y, cw[0], ys, xs), Spread(w1, y, x, cw[1], xs, ys)]
    ks = [
        Spread(k0, x, y, kpack.at[pl.ds(0, 144)], ys, xs),
        Spread(k1, y, x, kpack.at[pl.ds(144, 144)], xs, ys),
    ]
    m_c = net.copy(mb.at[h], mb.at[h], opposite)
    s_opp = {
        (g, v): net.copy(group(theirs, g, v), b.at[g, 0, 1], opposite)
        for g in (0, 1)
        for v, b in ((0, sk), (1, sv))
    }
    qf_opp = [
        net.copy(cols(q_hbm, theirs), qb.at[1], opposite),
        net.copy(cols(fresh_hbm, theirs), fk.at[1], opposite),
        net.copy(cols(fresh_hbm, D // 2 + theirs), fv.at[1], opposite),
    ]
    stale = {
        (r, g, v): Ring(
            net, lambda k, b=b, r=r, g=g: b.at[g, k, r], v, left, right
        )
        for r in (0, 1)
        for g in (0, 1)
        for v, b in ((0, sk), (1, sv))
    }
    stale_work = list(STALE)

    def pump(n):
        for _ in range(n):
            s, r, g = stale_work.pop(0)
            for v in (0, 1):
                if s > 0:
                    stale[r, g, v].forward(s)
                else:
                    if r == 1:
                        s_opp[g, v].wait_recv()
                    stale[r, g, v].start()

    def each(things, method, *args):
        for t in things:
            getattr(t, method)(*args)

    def tile(a, b, i, c, lo):
        return [jnp.concatenate([a[i, c, t], b[t, c, i]], axis=0) for t in (lo, 2 + lo)]

    held = {}

    def context():
        ctx = jnp.zeros((256, 384), F32)
        for i in range(NX):
            blocks = []
            for lo in (0, 1):
                for c in (0, 1):
                    a, b = tile(w0, w1, i, c, lo)
                    blocks.append(jnp.concatenate([a[0:128], b[0:128], a[128:], b[128:]], axis=0))
            rhs = jnp.concatenate(blocks, axis=1)
            text[i].finish()
            lhs = tx[i].reshape(256, 1024)
            ctx = ctx + lax.dot_general(
                lhs, rhs, (((1,), (1,)), ((), ())), preferred_element_type=F32
            )
        lane = lax.broadcasted_iota(jnp.int32, (256, 128), 1)
        s1 = jnp.sum(ctx, -1, keepdims=True)
        s2 = jnp.sum(ctx * ctx, -1, keepdims=True)
        both = jnp.where(lane == 0, s1, jnp.where(lane == 1, s2, 0.0))
        st[0] = jnp.transpose(both)[0:2]
        st_c = [net.copy(st.at[0], st.at[k], zs[k]) for k in zs]
        for c in st_c:
            c.start()
        held.update(ctx=ctx, st_c=st_c)

    def norm():
        ctx, st_c = held["ctx"], held["st_c"]
        m_c.wait_recv()
        low = lax.broadcasted_iota(jnp.int32, (8, 128), 1) < 64
        ma, mb_ = mb[0], mb[1]
        tail = jnp.where(low, ma[:, 128:256], pltpu.roll(mb_[:, 128:256], 64, 1))
        modul = jnp.concatenate([ma[:, 0:128], mb_[:, 0:128], tail], axis=1)
        for c in st_c:
            c.wait_recv()
        tot = st[0]
        for k in range(1, NZ):
            tot = tot + st[k]
        tot = jnp.transpose(jnp.concatenate([tot, jnp.zeros((126, 256), F32)], axis=0))
        average = tot[:, 0:1] / D
        variance = tot[:, 1:2] / D - average * average
        normed = (
            (ctx - average) * lax.rsqrt(variance + 1e-06) * (1.0 + modul[0:1]) + modul[1:2]
        ).astype(BF)
        held["normed"] = normed

    def partial_kv():
        normed = held["normed"]
        for i in range(NX):
            for lo in (0, 1):
                blocks = []
                for c in (0, 1):
                    a, b = tile(k0, k1, i, c, lo)
                    ra, rb = a[192:], b[192:]
                    last = jnp.concatenate(
                        [
                            jnp.concatenate([ra[:, 0:64], rb[:, 0:64]], axis=1),
                            jnp.concatenate([ra[:, 64:], rb[:, 64:]], axis=1),
                        ],
                        axis=0,
                    )
                    blocks.append(jnp.concatenate([a[0:192], b[0:192], last], axis=1))
                part = lax.dot_general(
                    normed,
                    jnp.concatenate(blocks, axis=0),
                    (((1,), (1,)), ((), ())),
                    preferred_element_type=F32,
                )
                at = (i * 2 + lo) * 384
                pt[:, :, at : at + 384] = part.reshape(NZ, 32, 384)

    parts = (slice(0, D // 2), slice(D // 2, D))
    steps = {}
    for n in range(4):
        for way in (0, 1):
            for p in (way, 1 - way):
                if n > 0 or p == way:
                    to = left if way == 0 else right
                    steps[n, way, p] = net.copy(rs_out.at[way, n, p], rs_in.at[way, n, p], to)

    def sum_step(n):
        for p in (0, 1):
            for way in (0, 1):
                if (n, way, p) not in steps:
                    continue
                term = pt[at_z(4 - n if way == 0 else 4 + n), :, parts[p]]
                if (n - 1, way, p) in steps:
                    steps[n - 1, way, p].wait_recv()
                    term = term + rs_in[way, n - 1, p]
                rs_out[way, n, p] = term.astype(BF)
                steps[n, way, p].start()

    tring = [
        Ring(net, lambda k, b=b, r=r: b.at[k, r], far, left, right)
        for r in (0, 1)
        for far, b in ((0, tk), (1, tv))
    ]
    t_opp = []

    def sum_end():
        for p, b in ((0, tk), (1, tv)):
            for way in (0, 1):
                steps[3, way, p].wait_recv()
            tkv[p] = (pt[z, :, parts[p]] + rs_in[0, 3, p] + rs_in[1, 3, p]).astype(BF)
            c = net.copy(tkv.at[p, :, pl.ds(pl.multiple_of(theirs, 128), HALF)], b.at[0, 1], opposite)
            c.start()
            t_opp.append(c)
            b[0, 0] = tkv[p, :, pl.ds(pl.multiple_of(mine, 128), HALF)]
            tring[p].start()

    def ring_opposite():
        for p in (0, 1):
            t_opp[p].wait_recv()
            tring[2 + p].start()

    c2 = math.log2(math.e) / math.sqrt(HEAD)
    contract = (((1,), (1,)), ((), ()))

    def head(n):
        return pl.ds(n * HEAD, HEAD)

    def scores(q, k):
        return lax.dot_general(q, k, contract, preferred_element_type=F32) * c2

    def first_block(g, n):
        for r in (0, 1):
            at = head(n - 3 * g)
            k = jnp.concatenate([fk[r, :, head(n)], sk[g, 0, 1 - r, :, at]], axis=0)
            v = jnp.concatenate([fv[r, :, head(n)], sv[g, 0, 1 - r, :, at]], axis=0)
            s = scores(qb[r, :, head(n)], k)
            m = jnp.max(s, -1, keepdims=True)
            p = jnp.exp2(s - m)
            rows = pl.ds(r * 128, 128)
            mx[n, rows] = jnp.broadcast_to(m, (128, 128))
            dn[n, rows] = jnp.broadcast_to(jnp.sum(p, -1, keepdims=True), (128, 128))
            acc[n, rows] = jnp.dot(p.astype(BF), v, preferred_element_type=F32)

    def attend(keys, values, mask=None, block=None, heads=(0, NH)):
        first = heads[0]
        rows = slice(None) if block is None else pl.ds(block * 128, 128)

        def body(n):
            if block is None:
                q = qb[:, :, head(n)].reshape(256, HEAD)
            else:
                q = qb[block, :, head(n)]
            k = jnp.concatenate([b[..., head(n - first)].reshape(-1, HEAD) for b in keys], axis=0)
            v = jnp.concatenate([b[..., head(n - first)].reshape(-1, HEAD) for b in values], axis=0)
            s = scores(q, k)
            if mask is not None:
                s = jnp.where(mask, s, -jnp.inf)
            old = mx[n, rows]
            m = jnp.maximum(old, jnp.max(s, -1, keepdims=True))
            p = jnp.exp2(s - m[:, 0:1])
            alpha = jnp.exp2(old - m)
            mx[n, rows] = m
            dn[n, rows] = dn[n, rows] * alpha + jnp.sum(p, -1, keepdims=True)
            acc[n, rows] = acc[n, rows] * alpha + jnp.dot(
                p.astype(BF), v, preferred_element_type=F32
            )

        for n in range(*heads):
            body(n)

    def attend_slots(g, *slots, block=None):
        attend(
            [sk.at[g, k] for k in slots],
            [sv.at[g, k] for k in slots],
            block=block,
            heads=(3 * g, 3 * g + 3),
        )

    def first():
        each(qf_opp, "wait_recv")
        for g in (0, 1):
            for n in range(3 * g, 3 * g + 3):
                first_block(g, n)

    def attend_text(*slots):
        n = len(slots) * 64
        at = lax.broadcasted_iota(jnp.int32, (1, n), 1)
        slot = jnp.full((1, n), slots[0], jnp.int32)
        for k in range(1, len(slots)):
            slot = jnp.where(at >= k * 64, slots[k], slot)
        position = at_z(slot) * 64 + jnp.where((at // 32) % 2 == 0, h, 1 - h) * 32 + at % 32
        attend([tk.at[k] for k in slots], [tv.at[k] for k in slots], position < len_ref[0])

    def out_cols(g):
        return cols(out_hbm, mine + g * GROUP, GROUP)

    o_c = [net.copy(ob.at[1, g], out_cols(g), opposite) for g in (0, 1)]
    own = []

    def finish(g):
        for r in (0, 1):
            for v in (0, 1):
                stale[r, g, v].finish()
        for block in (1, 0):
            attend_slots(g, 4, block=block)
            rows = pl.ds(block * 128, 128)
            for n in range(3):
                part = acc[3 * g + n, rows] / dn[3 * g + n, rows]
                ob[block, g, :, n * HEAD : (n + 1) * HEAD] = part.astype(BF)
            if block == 1:
                o_c[g].start()
            else:
                own.append(local(ob.at[0, g], out_cols(g)))

    ops = {
        "wf": lambda: each(ws, "finish"),
        "wp": lambda: each(ws, "pass_on"),
        "ws": lambda: each(ws, "start"),
        "wm": lambda: (each(c_cw, "wait"), each(ws, "middle")),
        "ks": lambda: each(ks, "start"),
        "km": lambda: each(ks, "middle"),
        "kp": lambda: each(ks, "pass_on"),
        "kf": lambda: each(ks, "finish"),
        "ms": m_c.start,
        "so": lambda: each(s_opp.values(), "start"),
        "qf": lambda: each(qf_opp, "start"),
        "T1": context,
        "NO": norm,
        "T2": partial_kv,
        "rf": sum_end,
        "to": ring_opposite,
        "P": lambda: pump(1),
        "PA": lambda: pump(len(stale_work)),
        "F0": lambda: finish(0),
        "F1": lambda: finish(1),
        "A0": first,
        "ts": lambda: each(text, "start"),
        "af": lambda: each(tring, "finish"),
    }
    for n in range(4):
        ops[f"r{n}"] = functools.partial(sum_step, n)
        ops[f"t{n}"] = functools.partial(each, text, "forward", n)
        ops[f"a{n}"] = functools.partial(each, tring, "forward", n)
        ops[f"b{n}"] = functools.partial(each, tring[0:2], "forward", n)
        ops[f"c{n}"] = functools.partial(each, tring[2:4], "forward", n)
    for op in PLAN:
        if op in ops:
            ops[op]()
        elif op[0] == "S":
            attend_slots(0, *map(int, op[1:]))
            attend_slots(1, *map(int, op[1:]))
        elif op[0] in "DE":
            attend_slots("DE".index(op[0]), *map(int, op[1:]))
        else:
            attend_text(*map(int, op[1:]))

    each(own, "wait")
    each(o_c, "wait_recv")
    net.drain()


N_COPIES = 224
STALE = (
    *((0, r, g) for r in (0, 1) for g in (0, 1)),
    *((s, r, g) for s in (1, 2, 3) for g in (0, 1) for r in (0, 1)),
)
PLAN = (
    "ts", "ws", "ms", "wm", "ks", "so", "t1", "t2", "P", "t3", "P", "wp",
    "km", "P", "P", "wf", "T1", "kp", "qf", "P", "P", "NO", "kf", "T2",
    "r0", "P", "r1", "P", "A0", "r2", "P", "r3", "P", "rf", "P", "to",
    "S17", "a1", "P", "X017", "a2", "P", "S26", "X26", "a3", "P", "PA", "S35",
    "af", "X354", "F0", "F1",
)


def per_device(img_q, fresh_kv, stale_kv, text_states, ctx_weight, kv_weight, modulation, lengths):
    hbm = pl.BlockSpec(memory_space=pltpu.HBM)
    smem = pl.BlockSpec(memory_space=pltpu.SMEM)
    return pl.pallas_call(
        kernel,
        out_shape=jax.ShapeDtypeStruct((1, 128, 1536), BF),
        in_specs=[hbm] * 7 + [smem],
        out_specs=hbm,
        scratch_shapes=[
            pltpu.VMEM((4, NZ, 32, 1024), BF),
            pltpu.VMEM((192, 192), BF),
            pltpu.VMEM((288, 128), BF),
            pltpu.VMEM((NX, 2, NY, 96, 256), BF),
            pltpu.VMEM((NY, 2, NX, 96, 256), BF),
            pltpu.VMEM((NX, 2, NY, 144, 128), BF),
            pltpu.VMEM((NY, 2, NX, 144, 128), BF),
            pltpu.VMEM((2, 192), F32),
            pltpu.VMEM((2, 8, 256), F32),
            pltpu.VMEM((NZ, 2, 256), F32),
            pltpu.VMEM((NZ, 32, D), F32),
            pltpu.VMEM((2, 4, 2, 32, D // 2), BF),
            pltpu.VMEM((2, 4, 2, 32, D // 2), BF),
            pltpu.VMEM((2, 32, D // 2), BF),
            pltpu.VMEM((NZ, 2, 32, HALF), BF),
            pltpu.VMEM((NZ, 2, 32, HALF), BF),
            pltpu.VMEM((2, NZ, 2, 128, GROUP), BF),
            pltpu.VMEM((2, NZ, 2, 128, GROUP), BF),
            pltpu.VMEM((2, 128, HALF), BF),
            pltpu.VMEM((2, 128, HALF), BF),
            pltpu.VMEM((2, 128, HALF), BF),
            pltpu.VMEM((NH, 256, HEAD), F32),
            pltpu.VMEM((NH, 256, HEAD), F32),
            pltpu.VMEM((NH, 256, HEAD), F32),
            pltpu.VMEM((2, 2, 128, HALF // 2), BF),
            pltpu.SemaphoreType.DMA((N_COPIES,)),
            pltpu.SemaphoreType.DMA((N_COPIES,)),
            pltpu.SemaphoreType.DMA((24,)),
        ],
        compiler_params=pltpu.CompilerParams(
            collective_id=0, has_side_effects=True, vmem_limit_bytes=58 << 20
        ),
    )(img_q, fresh_kv, stale_kv, text_states, ctx_weight.T, kv_weight, modulation, lengths)


def solution(mesh):
    in_specs = (
        P("img", "patch", None),
        P("img", "patch", None),
        P("img", "patch", None),
        P("img", "patch", None),
        P("img", "patch"),
        P("img", "patch"),
        P("img", None, "patch"),
        P("img"),
    )
    return jax.shard_map(
        per_device,
        mesh=mesh,
        in_specs=in_specs,
        out_specs=P("img", "patch", None),
        check_vma=False,
    )
```
